256 devices in a mesh: row: 64 (over z, x, core), col: 4 (over y).
Axes of the slice: x: 4, y: 4, z: 8, core: 2. Of those that a mesh axis runs over, the one named last changes fastest.
Arguments:
- features: bfloat16 [16384, 1024], P('row', 'col'), may hold values from -6 to 6
- masks: int32 [16384, 4, 1024], P('row', None, 'col'), may hold values 0 or 1
- adj_values: bfloat16 [512, 128, 128], P('row'), may hold values from 0.049804688 to 1
- adj_rows: int32 [512], P('row'), may hold values from 0 to 1, as said below
- adj_cols: int32 [512], P('row'), may hold values from 0 to 127, as said below
- adj_count: int32 [64], P('row'), may hold values from 6 to 8, as said below
- w_self_one: bfloat16 [1024, 1024], P('col'), may hold values from -0.1875 to 0.1875
- w_neigh_one: bfloat16 [1024, 1024], P('col'), may hold values from -0.1875 to 0.1875
- w_self_two: bfloat16 [1024, 1024], P('col'), may hold values from -0.1875 to 0.1875
- w_neigh_two: bfloat16 [1024, 1024], P('col'), may hold values from -0.1875 to 0.1875
Outputs:
- embeddings: bfloat16 [16384, 4, 1024], P('row', None, 'col')
The draws below stay inside these ranges and needn't reach their ends.
Inputs may be any that keep to these rules, and one draw needn't show every extreme that they name: `adj_rows`: slot k < 2 of each device has row block k and is that device's own diagonal block; the other slots' row blocks are any of the device's 2 blocks. `adj_cols`: A slot of device r names a column block of device r - 2, r - 1, r, r + 1 or r + 2 along row. `adj_count`: some device has all 8 slots live.
All inputs are finite; a program needn't handle non-finite values. No bound on the sum of `masks` on one device may be relied on, other than what follows from the above.
Results may differ from the reference program's by a relative error of at most 0.017.
Values may be sent and summed in bfloat16 or wider, within the bound.
A program may use at most 64 MiB of HBM per device.

```python
import math
import jax
import jax.numpy as jnp
from jax import lax

H = 1024
BS = 128
PASSES = 4
NB_DEV = 2
MAXB = 8
NODES = 16384
BLOCKS = 512
N_ROW = 64
N_COL = 4


def layout(key):
    keys = jax.random.split(key, 5)
    owner = jnp.arange(N_ROW, dtype=jnp.int32)[:, None]
    slot = jnp.arange(MAXB, dtype=jnp.int32)[None, :]
    pick_row = jax.random.randint(keys[0], (N_ROW, MAXB), 0, NB_DEV, dtype=jnp.int32)
    rows = jnp.where(slot < NB_DEV, slot, pick_row)
    rim_table = jnp.array([-2, -1, 1, 2], dtype=jnp.int32)
    rim_off = rim_table[jnp.clip(slot - NB_DEV, 0, 3)]
    rand_off = jax.random.randint(keys[1], (N_ROW, MAXB), -2, 3, dtype=jnp.int32)
    offset = jnp.where(slot < NB_DEV, 0, jnp.where(slot < NB_DEV + 4, rim_off, rand_off))
    rand_blk = jax.random.randint(keys[2], (N_ROW, MAXB), 0, NB_DEV, dtype=jnp.int32)
    block = jnp.where(slot < NB_DEV, slot, rand_blk)
    target = owner + offset
    valid = (target >= 0) & (target < N_ROW)
    cols = jnp.where(valid, target * NB_DEV + block, owner * NB_DEV + block)
    spare = MAXB - NB_DEV - 4
    draw_u = jax.random.randint(keys[3], (N_ROW,), 0, spare + 1, dtype=jnp.int32)
    count = NB_DEV + 4 + draw_u * draw_u * draw_u // (spare * spare)
    fullest = jax.random.randint(keys[4], (), 0, N_ROW, dtype=jnp.int32)
    count = jnp.where(jnp.arange(N_ROW, dtype=jnp.int32) == fullest, MAXB, count)
    return (rows.reshape(-1).astype(jnp.int32), cols.reshape(-1).astype(jnp.int32), count.astype(jnp.int32))


def draw_adj_rows(key, part):
    return layout(key)[0]


def draw_adj_cols(key, part):
    return layout(key)[1]


def draw_adj_count(key, part):
    return layout(key)[2]


def touch_ends(values, own_key, smallest, top_value):
    longest = values.shape.index(max(values.shape))
    spots = []
    for shift in (0, 1):
        where = [jax.random.randint(jax.random.fold_in(own_key, axis), (), 0, length) for axis, length in enumerate(values.shape)]
        where[longest] = (where[longest] + shift) % values.shape[longest]
        spots.append(tuple(where))
    return values.at[spots[0]].set(smallest).at[spots[1]].set(top_value)


def block_levels(stream_key, dims, cuts, smallest, largest):
    level = 1.0
    for dim, parts in cuts:
        heights = jax.random.uniform(jax.random.fold_in(jax.random.fold_in(stream_key, 6), dim), (parts,), jnp.float32, smallest / len(cuts), largest / len(cuts))
        level = level * jnp.repeat(jnp.exp(heights), dims[dim] // parts).reshape((-1,) + (1,) * (len(dims) - 1 - dim))
    return level


def bell_draw(key, dims, scale, reach, cuts=(), kind=jnp.bfloat16):
    gain = block_levels(key, dims, cuts, -0.22, 0.18) if cuts else 1.0
    values = jax.random.normal(key, dims, jnp.float32) * scale * gain
    return jnp.minimum(jnp.maximum(values, -reach), reach).astype(kind)


def setup_inputs(seed: int = 0) -> dict:
    key_of = jax.random.split(jax.random.key(seed), 11)
    return {
        "features": bell_draw(key_of[0], (NODES, H), 1.0, 6.0, ((0, 64), (1, 4))),
        "masks": touch_ends((jax.random.randint(key_of[1], (NODES, PASSES, H), 0, 2) < 1).astype(jnp.int32), jax.random.fold_in(key_of[1], 1), 0, 1),
        "adj_values": jnp.clip(jnp.exp(math.log(1.0) - 2.9996462 * jax.random.uniform(key_of[2], (BLOCKS, BS, BS), jnp.float32) ** block_levels(key_of[2], (BLOCKS, BS, BS), ((0, 64),), -0.2, 0.2)), 0.049804688, 1.0).astype(jnp.bfloat16),
        "adj_rows": draw_adj_rows(jax.random.fold_in(key_of[10], 71), 0),
        "adj_cols": draw_adj_cols(jax.random.fold_in(key_of[10], 71), 0),
        "adj_count": draw_adj_count(jax.random.fold_in(key_of[10], 71), 0),
        "w_self_one": bell_draw(key_of[6], (H, H), H ** -0.5, 0.1875, ((0, 4),)),
        "w_neigh_one": bell_draw(key_of[7], (H, H), H ** -0.5, 0.1875, ((0, 4),)),
        "w_self_two": bell_draw(key_of[8], (H, H), H ** -0.5, 0.1875, ((0, 4),)),
        "w_neigh_two": bell_draw(key_of[9], (H, H), H ** -0.5, 0.1875, ((0, 4),)),
    }


def aggregate(node_data, adj_values, adj_rows, adj_cols, adj_count):
    width = node_data.shape[1]
    tiles_all = node_data.reshape(NB_DEV * N_ROW, BS, width)

    def one_device(packed):
        values, rows, cols, count = packed
        live = jnp.arange(MAXB, dtype=jnp.int32) < count
        placing = ((rows[None, :] == jnp.arange(NB_DEV, dtype=jnp.int32)[:, None]) & live[None, :]).astype(jnp.float32)
        tiles = tiles_all[cols].astype(jnp.float32)
        values_wide = values.astype(jnp.float32)
        prods = jnp.einsum('sij,sjc->sic', values_wide, tiles, precision=lax.Precision.HIGHEST)
        summed = jnp.einsum('bs,sic->bic', placing, prods, precision=lax.Precision.HIGHEST)
        degree = jnp.dot(placing, lax.optimization_barrier(jnp.sum(values_wide, axis=2)), precision=lax.Precision.HIGHEST)
        return (summed * lax.rsqrt(degree)[:, :, None]).astype(jnp.bfloat16)
    stacked = lax.map(one_device, (adj_values.reshape(N_ROW, MAXB, BS, BS), adj_rows.reshape(N_ROW, MAXB), adj_cols.reshape(N_ROW, MAXB), adj_count))
    return stacked.reshape(NB_DEV * N_ROW * BS, width)

def project(inputs, agg, w_self, w_neigh):
    quarter = H // N_COL
    total = jnp.zeros((inputs.shape[0], H), jnp.float32)
    for part_index in range(N_COL):
        low = part_index * quarter
        high = low + quarter
        term = jnp.dot(inputs[:, low:high].astype(jnp.float32), w_self[low:high].astype(jnp.float32), precision=lax.Precision.HIGHEST)
        term = term + jnp.dot(agg[:, low:high].astype(jnp.float32), w_neigh[low:high].astype(jnp.float32), precision=lax.Precision.HIGHEST)
        rounded = lax.optimization_barrier(term.astype(jnp.bfloat16))
        total = total + rounded.astype(jnp.float32)
    return total

def reference(features, masks, adj_values, adj_rows, adj_cols, adj_count, w_self_one, w_neigh_one, w_self_two, w_neigh_two):
    first_agg = aggregate(features, adj_values, adj_rows, adj_cols, adj_count)
    hidden = jax.nn.relu(project(features, first_agg, w_self_one, w_neigh_one)).astype(jnp.bfloat16)
    dropped = hidden[:, None, :] * (2 * masks).astype(jnp.bfloat16)
    second_agg = aggregate(dropped.reshape(NODES, PASSES * H), adj_values, adj_rows, adj_cols, adj_count).reshape(NODES, PASSES, H)
    results = []
    for pass_index in range(PASSES):
        results.append(project(dropped[:, pass_index], second_agg[:, pass_index], w_self_two, w_neigh_two).astype(jnp.bfloat16))
    return jnp.stack(results, axis=1)
```

```python
import functools

import jax
import jax.numpy as jnp
from jax import lax
from jax.experimental import pallas as pl
from jax.experimental.pallas import tpu as pltpu
from jax.sharding import PartitionSpec as P

BS = 128
MESH = pl.DeviceIdType.MESH
ROW_OFFSETS = (2, -2, 1, -1)
COL_OFFSETS = (2, 1, 3)
BF16, F32 = jnp.bfloat16, jnp.float32


def fused(n_row, n_col, passes, blocks, slots, *refs):
    (features, masks, adj, adj_rows, adj_cols, adj_count, w_self_one, w_neigh_one,
     w_self_two, w_neigh_two, out) = refs[:11]
    rest = list(refs[11:])
    rows_s, cols_s, count_s, adj_v, placed, scale, ws1, wn1, ws2, wn2, mask_v = rest[:11]
    self_one, self_two, term_one, got_one, term_two, got_two, ext_one = rest[11:18]
    ext_two = rest[18:18 + passes]
    (load_sem, mask_sem, f_send, f_recv, d_send, d_recv, one_send, one_recv, two_send,
     two_recv) = rest[18 + passes:]

    r, c = lax.axis_index("row"), lax.axis_index("col")
    node_rows = blocks * BS

    def on_row(by):
        return (lax.rem(r + by + n_row, n_row), c)

    def on_col(by):
        return (r, lax.rem(c + by, n_col))

    barrier = pltpu.get_barrier_semaphore()
    for by in ROW_OFFSETS:
        pl.semaphore_signal(barrier, 1, device_id=on_row(by), device_id_type=MESH)
    for by in COL_OFFSETS:
        pl.semaphore_signal(barrier, 1, device_id=on_col(by), device_id_type=MESH)

    loads = []
    own = ext_one.at[pl.ds(2 * blocks, blocks)]
    for i, (src, dst) in enumerate(
        ((features, own), (adj, adj_v), (adj_rows, rows_s), (adj_cols, cols_s),
         (adj_count, count_s), (w_self_one, ws1), (w_neigh_one, wn1), (w_self_two, ws2),
         (w_neigh_two, wn2))
    ):
        loads.append(pltpu.make_async_copy(src, dst, load_sem.at[i]))
    mask_loads = [
        pltpu.make_async_copy(masks.at[:, p, :], mask_v.at[p], mask_sem.at[p])
        for p in range(passes)
    ]
    for copy in loads + mask_loads:
        copy.start()
    loads[0].wait()
    pl.semaphore_wait(barrier, len(ROW_OFFSETS) + len(COL_OFFSETS))

    def exchange(ext, send, recv):
        copies = []
        for i, by in enumerate(ROW_OFFSETS):
            copy = pltpu.make_async_remote_copy(
                src_ref=ext.at[pl.ds(2 * blocks, blocks)],
                dst_ref=ext.at[pl.ds((2 - by) * blocks, blocks)],
                send_sem=send.at[i], recv_sem=recv.at[i],
                device_id=on_row(by), device_id_type=MESH)
            copy.start()
            copies.append(copy)
        return copies

    f_copies = exchange(ext_one, f_send, f_recv)

    for copy in loads[1:5]:
        copy.wait()
    me = r * blocks - 2 * blocks
    local = [jnp.clip(cols_s[s] - me, 0, 5 * blocks - 1) for s in range(slots)]
    for s in range(slots):
        live = s < count_s[0]
        for b in range(blocks):
            here = jnp.logical_and(live, rows_s[s] == b)
            keep = jnp.where(here, 1.0, 0.0).astype(BF16)
            placed[pl.ds(b * BS, BS), pl.ds(s * BS, BS)] = adj_v[s] * keep
    degree = jnp.dot(placed[...], jnp.ones((slots * BS, 2 * BS), BF16),
                     preferred_element_type=F32)
    scale[...] = lax.rsqrt(degree)

    def aggregate(ext):
        tiles = jnp.concatenate([ext[i] for i in local], axis=0)
        summed = jnp.dot(placed[...], tiles, preferred_element_type=F32)
        return (summed * scale[...]).astype(BF16)

    width = node_rows

    def quarter(k):
        return pl.ds(pl.multiple_of(lax.rem(c + k, n_col) * width, width), width)

    def spread(agg, self_term, w_neigh, term, got, send, recv):
        copies = []
        for k in COL_OFFSETS + (0,):
            total = self_term[k] + jnp.dot(
                agg, w_neigh[:, quarter(k)], preferred_element_type=F32)
            term[k] = total.astype(BF16)
            if k:
                copy = pltpu.make_async_remote_copy(
                    src_ref=term.at[k], dst_ref=got.at[k - 1],
                    send_sem=send.at[k - 1], recv_sem=recv.at[k - 1],
                    device_id=on_col(k), device_id_type=MESH)
                copy.start()
                copies.append(copy)
        return copies

    def gathered(term, got):
        total = term[0].astype(F32)
        for k in range(1, n_col):
            total = total + got[k - 1].astype(F32)
        return total

    def self_project(own_ref, w_self, self_term):
        mine = jnp.concatenate([own_ref[2 * blocks + b] for b in range(blocks)], axis=0)
        for k in range(n_col):
            self_term[k] = jnp.dot(mine, w_self[:, quarter(k)], preferred_element_type=F32)

    loads[5].wait()
    self_project(ext_one, ws1, self_one)
    for copy in loads[6:]:
        copy.wait()
    for copy in f_copies:
        copy.wait_recv()
    one = spread(aggregate(ext_one), self_one, wn1, term_one, got_one, one_send, one_recv)
    for copy in mask_loads:
        copy.wait()
    for copy in one:
        copy.wait_recv()
    hidden = jnp.maximum(gathered(term_one, got_one), 0.0).astype(BF16)
    doubled = (hidden + hidden).astype(F32)
    d_copies = []
    for p in range(passes):
        dropped = (doubled * mask_v[p].astype(F32)).astype(BF16)
        for b in range(blocks):
            ext_two[p][2 * blocks + b] = dropped[b * BS:(b + 1) * BS]
        d_copies.append(exchange(ext_two[p], d_send.at[p], d_recv.at[p]))
    for p in range(passes):
        self_project(ext_two[p], ws2, self_two.at[p])
    two = []
    for p in range(passes):
        for copy in d_copies[p]:
            copy.wait_recv()
        two.append(spread(aggregate(ext_two[p]), self_two.at[p], wn2, term_two.at[p],
                          got_two.at[p], two_send.at[p], two_recv.at[p]))
    for p in range(passes):
        for copy in two[p]:
            copy.wait_recv()
        out[p] = gathered(term_two.at[p], got_two.at[p]).astype(BF16)
    for group in [f_copies, one] + d_copies + two:
        for copy in group:
            copy.wait_send()


def interleave(stacked, out):
    passes, rows, _ = stacked.shape
    step = 32
    for low in range(0, rows, step):
        part = stacked[:, low:low + step, :].astype(F32)
        out[low:low + step] = jnp.swapaxes(part, 0, 1).astype(BF16)


def solution(mesh):
    n_row, n_col = mesh.shape["row"], mesh.shape["col"]

    def on_device(features, masks, adj, adj_rows, adj_cols, adj_count, *weights):
        node_rows, width = features.shape
        blocks, slots, passes = node_rows // BS, adj_rows.shape[0], masks.shape[1]
        hidden = weights[0].shape[1]
        dma = pltpu.SemaphoreType.DMA
        tile = (node_rows, width)
        ext = pltpu.VMEM((5 * blocks, BS, width), BF16)
        any_spec = pl.BlockSpec(memory_space=pl.ANY)
        vmem_spec = pl.BlockSpec(memory_space=pltpu.VMEM)
        stacked = pl.pallas_call(
            functools.partial(fused, n_row, n_col, passes, blocks, slots),
            out_shape=jax.ShapeDtypeStruct((passes,) + tile, BF16),
            in_specs=[any_spec] * 10,
            out_specs=vmem_spec,
            scratch_shapes=[
                pltpu.SMEM((slots,), jnp.int32), pltpu.SMEM((slots,), jnp.int32),
                pltpu.SMEM((1,), jnp.int32),
                pltpu.VMEM(adj.shape, BF16), pltpu.VMEM((node_rows, slots * BS), BF16),
                pltpu.VMEM(tile, F32),
            ] + [pltpu.VMEM((width, hidden), BF16)] * 4 + [
                pltpu.VMEM((passes,) + tile, jnp.int32),
                pltpu.VMEM((n_col,) + tile, F32), pltpu.VMEM((passes, n_col) + tile, F32),
                pltpu.VMEM((n_col,) + tile, BF16), pltpu.VMEM((n_col - 1,) + tile, BF16),
                pltpu.VMEM((passes, n_col) + tile, BF16),
                pltpu.VMEM((passes, n_col - 1) + tile, BF16),
            ] + [ext] * (1 + passes) + [
                dma((9,)), dma((passes,)), dma((4,)), dma((4,)), dma((passes, 4)),
                dma((passes, 4)), dma((n_col - 1,)), dma((n_col - 1,)),
                dma((passes, n_col - 1)), dma((passes, n_col - 1)),
            ],
            compiler_params=pltpu.CompilerParams(
                collective_id=0, has_side_effects=True, vmem_limit_bytes=48 * 2**20),
        )(features.reshape(blocks, BS, width), masks, adj, adj_rows, adj_cols, adj_count, *weights)
        return pl.pallas_call(
            interleave,
            out_shape=jax.ShapeDtypeStruct((node_rows, passes, width), BF16),
            in_specs=[vmem_spec],
            out_specs=vmem_spec,
            compiler_params=pltpu.CompilerParams(vmem_limit_bytes=16 * 2**20),
        )(stacked)

    in_specs = (
        P("row", "col"), P("row", None, "col"), P("row", None, None), P("row"), P("row"),
        P("row"), P("col", None), P("col", None), P("col", None), P("col", None),
    )
    return jax.shard_map(on_device, mesh=mesh, in_specs=in_specs,
                         out_specs=P("row", None, "col"), check_vma=False)
```

```python
import functools

import jax
import jax.numpy as jnp
from jax import lax
from jax.experimental import pallas as pl
from jax.experimental.pallas import tpu as pltpu
from jax.sharding import PartitionSpec as P

BS = 128
MESH = pl.DeviceIdType.MESH
ROW_OFFSETS = (2, -2, 1, -1)
COL_OFFSETS = (2, 1, 3)
BF16, F32 = jnp.bfloat16, jnp.float32


def fused(n_row, n_col, passes, blocks, slots, *refs):
    (features, masks, adj, adj_rows, adj_cols, adj_count, w_self_one, w_neigh_one,
     w_self_two, w_neigh_two, out) = refs[:11]
    rest = list(refs[11:])
    rows_s, cols_s, count_s, adj_v, placed, scale, ws1, wn1, ws2, wn2, mask_v = rest[:11]
    self_one, self_two, term_one, got_one, term_two, got_two, ext_one = rest[11:18]
    ext_two = rest[18:18 + passes]
    (load_sem, mask_sem, f_send, f_recv, d_send, d_recv, one_send, one_recv, two_send,
     two_recv) = rest[18 + passes:]

    r, c = lax.axis_index("row"), lax.axis_index("col")
    node_rows = blocks * BS

    def on_row(by):
        return (lax.rem(r + by + n_row, n_row), c)

    def on_col(by):
        return (r, lax.rem(c + by, n_col))

    barrier = pltpu.get_barrier_semaphore()
    for by in ROW_OFFSETS:
        pl.semaphore_signal(barrier, 1, device_id=on_row(by), device_id_type=MESH)
    for by in COL_OFFSETS:
        pl.semaphore_signal(barrier, 1, device_id=on_col(by), device_id_type=MESH)

    loads = []
    own = ext_one.at[pl.ds(2 * blocks, blocks)]
    for i, (src, dst) in enumerate(
        ((features, own), (adj, adj_v), (adj_rows, rows_s), (adj_cols, cols_s),
         (adj_count, count_s), (w_self_one, ws1), (w_neigh_one, wn1), (w_self_two, ws2),
         (w_neigh_two, wn2))
    ):
        loads.append(pltpu.make_async_copy(src, dst, load_sem.at[i]))
    mask_loads = [
        pltpu.make_async_copy(masks.at[:, p, :], mask_v.at[p], mask_sem.at[p])
        for p in range(passes)
    ]
    for copy in loads + mask_loads:
        copy.start()
    loads[0].wait()
    pl.semaphore_wait(barrier, len(ROW_OFFSETS) + len(COL_OFFSETS))

    def exchange(ext, send, recv):
        copies = []
        for i, by in enumerate(ROW_OFFSETS):
            copy = pltpu.make_async_remote_copy(
                src_ref=ext.at[pl.ds(2 * blocks, blocks)],
                dst_ref=ext.at[pl.ds((2 - by) * blocks, blocks)],
                send_sem=send.at[i], recv_sem=recv.at[i],
                device_id=on_row(by), device_id_type=MESH)
            copy.start()
            copies.append(copy)
        return copies

    f_copies = exchange(ext_one, f_send, f_recv)

    for copy in loads[1:5]:
        copy.wait()
    me = r * blocks - 2 * blocks
    local = [jnp.clip(cols_s[s] - me, 0, 5 * blocks - 1) for s in range(slots)]
    for s in range(slots):
        live = s < count_s[0]
        for b in range(blocks):
            here = jnp.logical_and(live, rows_s[s] == b)
            keep = jnp.where(here, 1.0, 0.0).astype(BF16)
            placed[pl.ds(b * BS, BS), pl.ds(s * BS, BS)] = adj_v[s] * keep
    degree = jnp.dot(placed[...], jnp.ones((slots * BS, 2 * BS), BF16),
                     preferred_element_type=F32)
    scale[...] = lax.rsqrt(degree)

    def aggregate(ext):
        tiles = jnp.concatenate([ext[i] for i in local], axis=0)
        summed = jnp.dot(placed[...], tiles, preferred_element_type=F32)
        return (summed * scale[...]).astype(BF16)

    width = node_rows

    def quarter(k):
        return pl.ds(pl.multiple_of(lax.rem(c + k, n_col) * width, width), width)

    def spread(agg, self_term, w_neigh, term, got, send, recv):
        copies = []
        for k in COL_OFFSETS + (0,):
            total = self_term[k] + jnp.dot(
                agg, w_neigh[:, quarter(k)], preferred_element_type=F32)
            term[k] = total.astype(BF16)
            if k:
                copy = pltpu.make_async_remote_copy(
                    src_ref=term.at[k], dst_ref=got.at[k - 1],
                    send_sem=send.at[k - 1], recv_sem=recv.at[k - 1],
                    device_id=on_col(k), device_id_type=MESH)
                copy.start()
                copies.append(copy)
        return copies

    def gathered(term, got):
        total = term[0].astype(F32)
        for k in range(1, n_col):
            total = total + got[k - 1].astype(F32)
        return total

    def self_project(own_ref, w_self, self_term):
        mine = jnp.concatenate([own_ref[2 * blocks + b] for b in range(blocks)], axis=0)
        for k in range(n_col):
            self_term[k] = jnp.dot(mine, w_self[:, quarter(k)], preferred_element_type=F32)

    loads[5].wait()
    self_project(ext_one, ws1, self_one)
    for copy in loads[6:]:
        copy.wait()
    for copy in f_copies:
        copy.wait_recv()
    one = spread(aggregate(ext_one), self_one, wn1, term_one, got_one, one_send, one_recv)
    for copy in mask_loads:
        copy.wait()
    for copy in one:
        copy.wait_recv()
    hidden = jnp.maximum(gathered(term_one, got_one), 0.0).astype(BF16)
    doubled = (hidden + hidden).astype(F32)
    d_copies = []
    for p in range(passes):
        dropped = (doubled * mask_v[p].astype(F32)).astype(BF16)
        for b in range(blocks):
            ext_two[p][2 * blocks + b] = dropped[b * BS:(b + 1) * BS]
        d_copies.append(exchange(ext_two[p], d_send.at[p], d_recv.at[p]))
    for p in range(passes):
        self_project(ext_two[p], ws2, self_two.at[p])
    two = []
    for p in range(passes):
        for copy in d_copies[p]:
            copy.wait_recv()
        two.append(spread(aggregate(ext_two[p]), self_two.at[p], wn2, term_two.at[p],
                          got_two.at[p], two_send.at[p], two_recv.at[p]))
    for p in range(passes):
        for copy in two[p]:
            copy.wait_recv()
        out[p] = gathered(term_two.at[p], got_two.at[p]).astype(BF16)
    for group in [f_copies, one] + d_copies + two:
        for copy in group:
            copy.wait_send()


def interleave(stacked, out):
    passes, rows, _ = stacked.shape
    step = 32
    for low in range(0, rows, step):
        part = stacked[:, low:low + step, :].astype(F32)
        out[low:low + step] = jnp.swapaxes(part, 0, 1).astype(BF16)


def solution(mesh):
    n_row, n_col = mesh.shape["row"], mesh.shape["col"]

    def on_device(features, masks, adj, adj_rows, adj_cols, adj_count, *weights):
        node_rows, width = features.shape
        blocks, slots, passes = node_rows // BS, adj_rows.shape[0], masks.shape[1]
        hidden = weights[0].shape[1]
        dma = pltpu.SemaphoreType.DMA
        tile = (node_rows, width)
        ext = pltpu.VMEM((5 * blocks, BS, width), BF16)
        any_spec = pl.BlockSpec(memory_space=pl.ANY)
        vmem_spec = pl.BlockSpec(memory_space=pltpu.VMEM)
        stacked = pl.pallas_call(
            functools.partial(fused, n_row, n_col, passes, blocks, slots),
            out_shape=pltpu.VMEM((passes,) + tile, BF16),
            in_specs=[any_spec] * 10,
            out_specs=vmem_spec,
            scratch_shapes=[
                pltpu.SMEM((slots,), jnp.int32), pltpu.SMEM((slots,), jnp.int32),
                pltpu.SMEM((1,), jnp.int32),
                pltpu.VMEM(adj.shape, BF16), pltpu.VMEM((node_rows, slots * BS), BF16),
                pltpu.VMEM(tile, F32),
            ] + [pltpu.VMEM((width, hidden), BF16)] * 4 + [
                pltpu.VMEM((passes,) + tile, jnp.int32),
                pltpu.VMEM((n_col,) + tile, F32), pltpu.VMEM((passes, n_col) + tile, F32),
                pltpu.VMEM((n_col,) + tile, BF16), pltpu.VMEM((n_col - 1,) + tile, BF16),
                pltpu.VMEM((passes, n_col) + tile, BF16),
                pltpu.VMEM((passes, n_col - 1) + tile, BF16),
            ] + [ext] * (1 + passes) + [
                dma((9,)), dma((passes,)), dma((4,)), dma((4,)), dma((passes, 4)),
                dma((passes, 4)), dma((n_col - 1,)), dma((n_col - 1,)),
                dma((passes, n_col - 1)), dma((passes, n_col - 1)),
            ],
            compiler_params=pltpu.CompilerParams(
                collective_id=0, has_side_effects=True, vmem_limit_bytes=48 * 2**20),
        )(*[pltpu.with_memory_space_constraint(x, pltpu.HBM) if x.size > 1 else x for x in (
            features.reshape(blocks, BS, width), masks, adj, adj_rows, adj_cols, adj_count, *weights)])
        return pl.pallas_call(
            interleave,
            out_shape=jax.ShapeDtypeStruct((node_rows, passes, width), BF16),
            in_specs=[vmem_spec],
            out_specs=vmem_spec,
            compiler_params=pltpu.CompilerParams(vmem_limit_bytes=16 * 2**20),
        )(stacked)

    in_specs = (
        P("row", "col"), P("row", None, "col"), P("row", None, None), P("row"), P("row"),
        P("row"), P("col", None), P("col", None), P("col", None), P("col", None),
    )
    return jax.shard_map(on_device, mesh=mesh, in_specs=in_specs,
                         out_specs=P("row", None, "col"), check_vma=False)
```

```python
import functools

import jax
import jax.numpy as jnp
from jax import lax
from jax.experimental import pallas as pl
from jax.experimental.pallas import tpu as pltpu
from jax.sharding import PartitionSpec as P

BS = 128
MESH = pl.DeviceIdType.MESH
BF16, F32 = jnp.bfloat16, jnp.float32


def fused(n_row, n_col, passes, blocks, slots, *refs):
    (features, masks, adj, adj_rows, adj_cols, adj_count, w_self_one, w_neigh_one,
     w_self_two, w_neigh_two, out) = refs[:11]
    rest = list(refs[11:])
    rows_s, cols_s, count_s, adj_v, placed, scale, ws1, wn1, ws2, wn2, mask_v = rest[:11]
    self_term, term, mid, relayed, got = rest[11:16]
    ext = rest[16:17 + passes]
    load_sem, mask_sem, row_send, row_recv, col_send, col_recv = rest[17 + passes:]

    r, c = lax.axis_index("row"), lax.axis_index("col")
    odd = lax.rem(r, 2)
    has_left, has_right = r >= 2, r < n_row - 2
    inner = jnp.where(odd == 0, has_right, has_left)
    outer = jnp.where(odd == 0, has_left, has_right)
    sibling = (r + 1 - 2 * odd, c)
    far_right, far_left = (lax.rem(r + 2, n_row), c), (lax.rem(r + n_row - 2, n_row), c)
    col_right, col_left = (r, lax.rem(c + 1, n_col)), (r, lax.rem(c + n_col - 1, n_col))
    node_rows = blocks * BS
    half = node_rows // 2

    barrier = pltpu.get_barrier_semaphore()

    def greet(device):
        pl.semaphore_signal(barrier, 1, device_id=device, device_id_type=MESH)

    pl.when(has_right)(lambda: greet(far_right))
    pl.when(has_left)(lambda: greet(far_left))
    for device in (sibling, col_right, col_left):
        greet(device)

    loads = []
    own = ext[0].at[pl.ds(2 * blocks, blocks)]
    for i, (src, dst) in enumerate(
        ((features, own), (adj, adj_v), (adj_rows, rows_s), (adj_cols, cols_s),
         (adj_count, count_s), (w_self_one, ws1), (w_neigh_one, wn1), (w_self_two, ws2),
         (w_neigh_two, wn2))
    ):
        loads.append(pltpu.make_async_copy(src, dst, load_sem.at[i]))
    mask_loads = [
        pltpu.make_async_copy(masks.at[:, p, :], mask_v.at[p], mask_sem.at[p])
        for p in range(passes)
    ]
    for copy in loads + mask_loads:
        copy.start()
    loads[0].wait()
    pl.semaphore_wait(barrier, 3 + has_left.astype(jnp.int32) + has_right.astype(jnp.int32))

    def remote(src, dst, send, recv, device):
        return pltpu.make_async_remote_copy(
            src_ref=src, dst_ref=dst, send_sem=send, recv_sem=recv, device_id=device,
            device_id_type=MESH)

    def row_copy(stage, i):
        src, dst, device = (
            (2, 0, far_right), (2, 4, far_left), (2, 1 + 2 * odd, sibling),
            (4 - 4 * odd, 3 - 2 * odd, sibling))[i]
        pairs = [ext[stage].at[pl.ds(n * blocks, blocks)] for n in (src, dst)]
        return remote(*pairs, row_send.at[stage, i], row_recv.at[stage, i], device)

    def row_start(stage):
        pl.when(has_right)(lambda: row_copy(stage, 0).start())
        pl.when(has_left)(lambda: row_copy(stage, 1).start())
        row_copy(stage, 2).start()

    def row_wait(stage):
        pl.when(has_left)(lambda: row_copy(stage, 0).wait_recv())
        pl.when(has_right)(lambda: row_copy(stage, 1).wait_recv())
        pl.when(inner)(lambda: row_copy(stage, 3).start())
        row_copy(stage, 2).wait_recv()
        pl.when(outer)(lambda: row_copy(stage, 3).wait_recv())

    def row_drain(stage):
        pl.when(has_right)(lambda: row_copy(stage, 0).wait_send())
        pl.when(has_left)(lambda: row_copy(stage, 1).wait_send())
        row_copy(stage, 2).wait_send()
        pl.when(inner)(lambda: row_copy(stage, 3).wait_send())

    top, low = pl.ds(0, half), pl.ds(half, half)

    def col_copy(stage, i):
        t, m, y, g = term.at[stage], mid.at[stage], relayed.at[stage], got.at[stage]
        src, dst, device = (
            (t.at[2, top], m.at[0], col_right), (t.at[2, low], m.at[1], col_left),
            (t.at[1, low], g.at[0, low], col_right), (t.at[3, top], g.at[1, top], col_left),
            (y.at[0], g.at[0, top], col_right), (y.at[1], g.at[1, low], col_left))[i]
        return remote(src, dst, col_send.at[stage, i], col_recv.at[stage, i], device)

    row_start(0)
    for copy in loads[1:5]:
        copy.wait()
    me = r * blocks - 2 * blocks
    local = [jnp.clip(cols_s[s] - me, 0, 5 * blocks - 1) for s in range(slots)]
    for s in range(slots):
        live = s < count_s[0]
        for b in range(blocks):
            here = jnp.logical_and(live, rows_s[s] == b)
            keep = jnp.where(here, 1.0, 0.0).astype(BF16)
            placed[pl.ds(b * BS, BS), pl.ds(s * BS, BS)] = adj_v[s] * keep
    degree = jnp.dot(placed[...], jnp.ones((slots * BS, 2 * BS), BF16),
                     preferred_element_type=F32)
    scale[...] = lax.rsqrt(degree)

    def aggregate(stage):
        tiles = jnp.concatenate([ext[stage][i] for i in local], axis=0)
        summed = jnp.dot(placed[...], tiles, preferred_element_type=F32)
        return (summed * scale[...]).astype(BF16)

    def quarter(k):
        return pl.ds(pl.multiple_of(lax.rem(c + k, n_col) * node_rows, node_rows), node_rows)

    def self_project(stage, w_self):
        mine = jnp.concatenate([ext[stage][2 * blocks + b] for b in range(blocks)], axis=0)
        for k in range(n_col):
            self_term[stage, k] = jnp.dot(mine, w_self[:, quarter(k)],
                                          preferred_element_type=F32)

    def spread(stage, w_neigh):
        agg = aggregate(stage)
        for k, sent in ((2, (0, 1)), (1, (2,)), (3, (3,)), (0, ())):
            total = self_term[stage, k] + jnp.dot(
                agg, w_neigh[:, quarter(k)], preferred_element_type=F32)
            term[stage, k] = total.astype(BF16)
            for i in sent:
                col_copy(stage, i).start()

    def relay(stage):
        for i, mine in ((0, term[stage, 1, top]), (1, term[stage, 3, low])):
            col_copy(stage, i).wait_recv()
            both = mine.astype(F32) + mid[stage, i].astype(F32)
            relayed[stage, i] = both.astype(BF16)
            col_copy(stage, 4 + i).start()

    def gathered(stage):
        for i in range(2, 6):
            col_copy(stage, i).wait_recv()
        return (term[stage, 0].astype(F32) + got[stage, 0].astype(F32)
                + got[stage, 1].astype(F32))

    loads[5].wait()
    self_project(0, ws1)
    for copy in loads[6:]:
        copy.wait()
    row_wait(0)
    spread(0, wn1)
    for copy in mask_loads:
        copy.wait()
    relay(0)
    hidden = jnp.maximum(gathered(0), 0.0).astype(BF16)
    doubled = (hidden + hidden).astype(F32)
    for p in range(passes):
        dropped = (doubled * mask_v[p].astype(F32)).astype(BF16)
        for b in range(blocks):
            ext[1 + p][2 * blocks + b] = dropped[b * BS:(b + 1) * BS]
        row_start(1 + p)
    for p in range(passes):
        self_project(1 + p, ws2)
    for p in range(passes):
        row_wait(1 + p)
        spread(1 + p, wn2)
        if p:
            relay(p)
    for p in range(passes):
        if p == passes - 2:
            relay(passes)
        out[p] = gathered(1 + p).astype(BF16)
    for stage in range(1 + passes):
        row_drain(stage)
        for i in range(6):
            col_copy(stage, i).wait_send()


def interleave(stacked, out):
    passes, rows, _ = stacked.shape
    step = 32
    for low in range(0, rows, step):
        part = stacked[:, low:low + step, :].astype(F32)
        out[low:low + step] = jnp.swapaxes(part, 0, 1).astype(BF16)


def solution(mesh):
    n_row, n_col = mesh.shape["row"], mesh.shape["col"]

    def on_device(features, masks, adj, adj_rows, adj_cols, adj_count, *weights):
        node_rows, width = features.shape
        blocks, slots, passes = node_rows // BS, adj_rows.shape[0], masks.shape[1]
        hidden = weights[0].shape[1]
        dma = pltpu.SemaphoreType.DMA
        tile, halved = (node_rows, width), (node_rows // 2, width)
        ext = pltpu.VMEM((5 * blocks, BS, width), BF16)
        any_spec = pl.BlockSpec(memory_space=pl.ANY)
        vmem_spec = pl.BlockSpec(memory_space=pltpu.VMEM)
        stacked = pl.pallas_call(
            functools.partial(fused, n_row, n_col, passes, blocks, slots),
            out_shape=pltpu.VMEM((passes,) + tile, BF16),
            in_specs=[any_spec] * 10,
            out_specs=vmem_spec,
            scratch_shapes=[
                pltpu.SMEM((slots,), jnp.int32), pltpu.SMEM((slots,), jnp.int32),
                pltpu.SMEM((1,), jnp.int32),
                pltpu.VMEM(adj.shape, BF16), pltpu.VMEM((node_rows, slots * BS), BF16),
                pltpu.VMEM(tile, F32),
            ] + [pltpu.VMEM((width, hidden), BF16)] * 4 + [
                pltpu.VMEM((passes,) + tile, jnp.int32),
                pltpu.VMEM((1 + passes, n_col) + tile, F32),
                pltpu.VMEM((1 + passes, n_col) + tile, BF16),
                pltpu.VMEM((1 + passes, 2) + halved, BF16),
                pltpu.VMEM((1 + passes, 2) + halved, BF16),
                pltpu.VMEM((1 + passes, 2) + tile, BF16),
            ] + [ext] * (1 + passes) + [
                dma((9,)), dma((passes,)), dma((1 + passes, 4)), dma((1 + passes, 4)),
                dma((1 + passes, 6)), dma((1 + passes, 6)),
            ],
            compiler_params=pltpu.CompilerParams(
                collective_id=0, has_side_effects=True, vmem_limit_bytes=48 * 2**20),
        )(*[pltpu.with_memory_space_constraint(x, pltpu.HBM) if x.size > 1 else x for x in (
            features.reshape(blocks, BS, width), masks, adj, adj_rows, adj_cols, adj_count, *weights)])
        return pl.pallas_call(
            interleave,
            out_shape=jax.ShapeDtypeStruct((node_rows, passes, width), BF16),
            in_specs=[vmem_spec],
            out_specs=vmem_spec,
            compiler_params=pltpu.CompilerParams(vmem_limit_bytes=16 * 2**20),
        )(stacked)

    in_specs = (
        P("row", "col"), P("row", None, "col"), P("row", None, None), P("row"), P("row"),
        P("row"), P("col", None), P("col", None), P("col", None), P("col", None),
    )
    return jax.shard_map(on_device, mesh=mesh, in_specs=in_specs,
                         out_specs=P("row", None, "col"), check_vma=False)
```

```python
import functools

import jax
import jax.numpy as jnp
from jax import lax
from jax.experimental import pallas as pl
from jax.experimental.pallas import tpu as pltpu
from jax.sharding import PartitionSpec as P

BS = 128
MESH = pl.DeviceIdType.MESH
BF16, F32 = jnp.bfloat16, jnp.float32


def fused(n_row, n_col, passes, blocks, slots, *refs):
    (features, masks, adj, adj_rows, adj_cols, adj_count, w_self_one, w_neigh_one,
     w_self_two, w_neigh_two, out) = refs[:11]
    rest = list(refs[11:])
    rows_s, cols_s, count_s, adj_v, placed, scale, ws1, wn1, ws2, wn2, mask_v = rest[:11]
    self_term, term, mid, relayed, got = rest[11:16]
    ext = rest[16:17 + passes]
    load_sem, mask_sem, row_send, row_recv, col_send, col_recv = rest[17 + passes:]

    r, c = lax.axis_index("row"), lax.axis_index("col")
    odd = lax.rem(r, 2)
    has_left, has_right = r >= 2, r < n_row - 2
    inner = jnp.where(odd == 0, has_right, has_left)
    outer = jnp.where(odd == 0, has_left, has_right)
    sibling = (r + 1 - 2 * odd, c)
    far_right, far_left = (lax.rem(r + 2, n_row), c), (lax.rem(r + n_row - 2, n_row), c)
    col_right, col_left = (r, lax.rem(c + 1, n_col)), (r, lax.rem(c + n_col - 1, n_col))
    neigh_stage, self_stage = passes, passes + 1
    node_rows = blocks * BS
    half = node_rows // 2

    barrier = pltpu.get_barrier_semaphore()

    def greet(device):
        pl.semaphore_signal(barrier, 1, device_id=device, device_id_type=MESH)

    pl.when(has_right)(lambda: greet(far_right))
    pl.when(has_left)(lambda: greet(far_left))
    for device in (sibling, col_right, col_left):
        greet(device)

    loads = []
    own = ext[0].at[pl.ds(2 * blocks, blocks)]
    for i, (src, dst) in enumerate(
        ((features, own), (adj, adj_v), (adj_rows, rows_s), (adj_cols, cols_s),
         (adj_count, count_s), (w_self_one, ws1), (w_neigh_one, wn1), (w_self_two, ws2),
         (w_neigh_two, wn2))
    ):
        loads.append(pltpu.make_async_copy(src, dst, load_sem.at[i]))
    mask_loads = [
        pltpu.make_async_copy(masks.at[:, p, :], mask_v.at[p], mask_sem.at[p])
        for p in range(passes)
    ]
    for copy in loads + mask_loads:
        copy.start()
    loads[0].wait()
    pl.semaphore_wait(barrier, 3 + has_left.astype(jnp.int32) + has_right.astype(jnp.int32))

    def remote(src, dst, send, recv, device):
        return pltpu.make_async_remote_copy(
            src_ref=src, dst_ref=dst, send_sem=send, recv_sem=recv, device_id=device,
            device_id_type=MESH)

    def row_copy(stage, i):
        src, dst, device = (
            (2, 0, far_right), (2, 4, far_left), (2, 1 + 2 * odd, sibling),
            (4 - 4 * odd, 3 - 2 * odd, sibling))[i]
        pairs = [ext[stage].at[pl.ds(n * blocks, blocks)] for n in (src, dst)]
        return remote(*pairs, row_send.at[stage, i], row_recv.at[stage, i], device)

    def row_start(stage):
        pl.when(has_right)(lambda: row_copy(stage, 0).start())
        pl.when(has_left)(lambda: row_copy(stage, 1).start())
        row_copy(stage, 2).start()

    def row_wait(stage):
        pl.when(has_left)(lambda: row_copy(stage, 0).wait_recv())
        pl.when(has_right)(lambda: row_copy(stage, 1).wait_recv())
        pl.when(inner)(lambda: row_copy(stage, 3).start())
        row_copy(stage, 2).wait_recv()
        pl.when(outer)(lambda: row_copy(stage, 3).wait_recv())

    def row_drain(stage):
        pl.when(has_right)(lambda: row_copy(stage, 0).wait_send())
        pl.when(has_left)(lambda: row_copy(stage, 1).wait_send())
        row_copy(stage, 2).wait_send()
        pl.when(inner)(lambda: row_copy(stage, 3).wait_send())

    top, low = pl.ds(0, half), pl.ds(half, half)

    def col_copy(stage, i):
        t, m, y, g = term.at[stage], mid.at[stage], relayed.at[stage], got.at[stage]
        src, dst, device = (
            (t.at[2, top], m.at[0], col_right), (t.at[2, low], m.at[1], col_left),
            (t.at[1, low], g.at[0, low], col_right), (t.at[3, top], g.at[1, top], col_left),
            (y.at[0], g.at[0, top], col_right), (y.at[1], g.at[1, low], col_left))[i]
        return remote(src, dst, col_send.at[stage, i], col_recv.at[stage, i], device)

    row_start(0)
    for copy in loads[1:5]:
        copy.wait()
    me = r * blocks - 2 * blocks
    local = [jnp.clip(cols_s[s] - me, 0, 5 * blocks - 1) for s in range(slots)]
    for s in range(slots):
        live = s < count_s[0]
        for b in range(blocks):
            here = jnp.logical_and(live, rows_s[s] == b)
            keep = jnp.where(here, 1.0, 0.0).astype(BF16)
            placed[pl.ds(b * BS, BS), pl.ds(s * BS, BS)] = adj_v[s] * keep
    degree = jnp.dot(placed[...], jnp.ones((slots * BS, 2 * BS), BF16),
                     preferred_element_type=F32)
    scale[...] = lax.rsqrt(degree)

    def aggregate(stage):
        tiles = jnp.concatenate([ext[stage][i] for i in local], axis=0)
        summed = jnp.dot(placed[...], tiles, preferred_element_type=F32)
        return summed * scale[...]

    def quarter(k):
        return pl.ds(pl.multiple_of(lax.rem(c + k, n_col) * node_rows, node_rows), node_rows)

    def own_rows(stage):
        return jnp.concatenate([ext[stage][2 * blocks + b] for b in range(blocks)], axis=0)

    def product(left, weight, k):
        return jnp.dot(left, weight[:, quarter(k)], preferred_element_type=F32)

    def self_project(stage, w_self):
        mine = own_rows(stage)
        for k in range(n_col):
            self_term[stage, k] = product(mine, w_self, k)

    def spread(stage, share):
        for k, sent in ((2, (0, 1)), (1, (2,)), (3, (3,)), (0, ())):
            term[stage, k] = share(k).astype(BF16)
            for i in sent:
                col_copy(stage, i).start()

    def spread_terms(row_stage, col_stage, w_neigh):
        row_wait(row_stage)
        agg = aggregate(row_stage).astype(BF16)
        spread(col_stage, lambda k: self_term[row_stage, k] + product(agg, w_neigh, k))

    def relay(stage):
        for i, mine in ((0, term[stage, 1, top]), (1, term[stage, 3, low])):
            col_copy(stage, i).wait_recv()
            both = mine.astype(F32) + mid[stage, i].astype(F32)
            relayed[stage, i] = both.astype(BF16)
            col_copy(stage, 4 + i).start()

    def gathered(stage):
        for i in range(2, 6):
            col_copy(stage, i).wait_recv()
        return (term[stage, 0].astype(F32) + got[stage, 0].astype(F32)
                + got[stage, 1].astype(F32))

    loads[5].wait()
    self_project(0, ws1)
    for copy in loads[6:]:
        copy.wait()
    spread_terms(0, 0, wn1)
    for copy in mask_loads:
        copy.wait()
    relay(0)
    hidden = jnp.maximum(gathered(0), 0.0).astype(BF16)
    doubled = (hidden + hidden).astype(F32)

    def dropped(p):
        return (doubled * mask_v[p].astype(F32)).astype(BF16)

    def send_rows(stage, value):
        for b in range(blocks):
            ext[stage][2 * blocks + b] = value[b * BS:(b + 1) * BS]
        row_start(stage)

    send_rows(1, dropped(1))
    first = dropped(0)
    spread(neigh_stage, lambda k: product(first, wn2, k))
    spread(self_stage, lambda k: product(first, ws2, k))
    for p in range(2, passes):
        send_rows(p, dropped(p))
    for p in range(1, passes):
        self_project(p, ws2)
    relay(neigh_stage)
    relay(self_stage)
    for p in range(1, passes):
        spread_terms(p, p, wn2)
        if p == 1:
            send_rows(passes, gathered(neigh_stage).astype(BF16))
        else:
            relay(p - 1)
    row_wait(passes)
    out[0] = (gathered(self_stage) + aggregate(passes)).astype(BF16)
    for p in range(1, passes):
        if p == passes - 2:
            relay(passes - 1)
        out[p] = gathered(p).astype(BF16)
    for stage in range(1 + passes):
        row_drain(stage)
    for stage in range(2 + passes):
        for i in range(6):
            col_copy(stage, i).wait_send()


def interleave(stacked, out):
    passes, rows, _ = stacked.shape
    step = 32
    for low in range(0, rows, step):
        part = stacked[:, low:low + step, :].astype(F32)
        out[low:low + step] = jnp.swapaxes(part, 0, 1).astype(BF16)


def solution(mesh):
    n_row, n_col = mesh.shape["row"], mesh.shape["col"]

    def on_device(features, masks, adj, adj_rows, adj_cols, adj_count, *weights):
        node_rows, width = features.shape
        blocks, slots, passes = node_rows // BS, adj_rows.shape[0], masks.shape[1]
        hidden = weights[0].shape[1]
        dma = pltpu.SemaphoreType.DMA
        tile, halved = (node_rows, width), (node_rows // 2, width)
        ext = pltpu.VMEM((5 * blocks, BS, width), BF16)
        any_spec = pl.BlockSpec(memory_space=pl.ANY)
        vmem_spec = pl.BlockSpec(memory_space=pltpu.VMEM)
        stacked = pl.pallas_call(
            functools.partial(fused, n_row, n_col, passes, blocks, slots),
            out_shape=pltpu.VMEM((passes,) + tile, BF16),
            in_specs=[any_spec] * 10,
            out_specs=vmem_spec,
            scratch_shapes=[
                pltpu.SMEM((slots,), jnp.int32), pltpu.SMEM((slots,), jnp.int32),
                pltpu.SMEM((1,), jnp.int32),
                pltpu.VMEM(adj.shape, BF16), pltpu.VMEM((node_rows, slots * BS), BF16),
                pltpu.VMEM(tile, F32),
            ] + [pltpu.VMEM((width, hidden), BF16)] * 4 + [
                pltpu.VMEM((passes,) + tile, jnp.int32),
                pltpu.VMEM((passes, n_col) + tile, F32),
                pltpu.VMEM((2 + passes, n_col) + tile, BF16),
                pltpu.VMEM((2 + passes, 2) + halved, BF16),
                pltpu.VMEM((2 + passes, 2) + halved, BF16),
                pltpu.VMEM((2 + passes, 2) + tile, BF16),
            ] + [ext] * (1 + passes) + [
                dma((9,)), dma((passes,)), dma((1 + passes, 4)), dma((1 + passes, 4)),
                dma((2 + passes, 6)), dma((2 + passes, 6)),
            ],
            compiler_params=pltpu.CompilerParams(
                collective_id=0, has_side_effects=True, vmem_limit_bytes=48 * 2**20),
        )(*[pltpu.with_memory_space_constraint(x, pltpu.HBM) if x.size > 1 else x for x in (
            features.reshape(blocks, BS, width), masks, adj, adj_rows, adj_cols, adj_count, *weights)])
        return pl.pallas_call(
            interleave,
            out_shape=jax.ShapeDtypeStruct((node_rows, passes, width), BF16),
            in_specs=[vmem_spec],
            out_specs=vmem_spec,
            compiler_params=pltpu.CompilerParams(vmem_limit_bytes=16 * 2**20),
        )(stacked)

    in_specs = (
        P("row", "col"), P("row", None, "col"), P("row", None, None), P("row"), P("row"),
        P("row"), P("col", None), P("col", None), P("col", None), P("col", None),
    )
    return jax.shard_map(on_device, mesh=mesh, in_specs=in_specs,
                         out_specs=P("row", None, "col"), check_vma=False)
```

```python
import functools

import jax
import jax.numpy as jnp
from jax import lax
from jax.experimental import pallas as pl
from jax.experimental.pallas import tpu as pltpu
from jax.sharding import PartitionSpec as P

BS = 128
MESH = pl.DeviceIdType.MESH
BF16, F32 = jnp.bfloat16, jnp.float32


def fused(n_row, n_col, passes, wide, blocks, slots, *refs):
    (features, masks, adj, adj_rows, adj_cols, adj_count, w_self_one, w_neigh_one,
     w_self_two, w_neigh_two, out) = refs[:11]
    rest = list(refs[11:])
    rows_s, cols_s, count_s, adj_v, placed, scale, ws1, wn1, w2, mask_v = rest[:10]
    self_term, term, mid, relayed, got, spread_w, shared, self_wide = rest[10:18]
    ext = rest[18:19 + passes]
    (load_sem, mask_sem, row_send, row_recv, col_send, col_recv, share_send, share_recv,
     w_send, w_recv) = rest[19 + passes:]

    r, c = lax.axis_index("row"), lax.axis_index("col")
    odd = lax.rem(r, 2)
    has_left, has_right = r >= 2, r < n_row - 2
    inner = jnp.where(odd == 0, has_right, has_left)
    outer = jnp.where(odd == 0, has_left, has_right)
    sibling = (r + 1 - 2 * odd, c)
    far_right, far_left = (lax.rem(r + 2, n_row), c), (lax.rem(r + n_row - 2, n_row), c)
    col_right, col_left = (r, lax.rem(c + 1, n_col)), (r, lax.rem(c + n_col - 1, n_col))
    narrow = range(wide, passes)
    col_across = (r, lax.rem(c + 2, n_col))
    node_rows = blocks * BS
    half = node_rows // 2

    barrier = pltpu.get_barrier_semaphore()

    def greet(device):
        pl.semaphore_signal(barrier, 1, device_id=device, device_id_type=MESH)

    pl.when(has_right)(lambda: greet(far_right))
    pl.when(has_left)(lambda: greet(far_left))
    for device in (sibling, col_right, col_left, col_across):
        greet(device)

    loads = []
    own = ext[0].at[pl.ds(2 * blocks, blocks)]
    for i, (src, dst) in enumerate(
        ((features, own), (adj, adj_v), (adj_rows, rows_s), (adj_cols, cols_s),
         (adj_count, count_s), (w_self_one, ws1), (w_neigh_one, wn1), (w_self_two, w2.at[0]),
         (w_neigh_two, w2.at[1]))
    ):
        loads.append(pltpu.make_async_copy(src, dst, load_sem.at[i]))
    mask_loads = [
        pltpu.make_async_copy(masks.at[:, p, :], mask_v.at[p], mask_sem.at[p])
        for p in range(passes)
    ]
    for copy in loads + mask_loads:
        copy.start()
    loads[0].wait()
    pl.semaphore_wait(barrier, 4 + has_left.astype(jnp.int32) + has_right.astype(jnp.int32))

    def remote(src, dst, send, recv, device):
        return pltpu.make_async_remote_copy(
            src_ref=src, dst_ref=dst, send_sem=send, recv_sem=recv, device_id=device,
            device_id_type=MESH)

    def row_copy(stage, i):
        src, dst, device = (
            (2, 0, far_right), (2, 4, far_left), (2, 1 + 2 * odd, sibling),
            (4 - 4 * odd, 3 - 2 * odd, sibling))[i]
        pairs = [ext[stage].at[pl.ds(n * blocks, blocks)] for n in (src, dst)]
        return remote(*pairs, row_send.at[stage, i], row_recv.at[stage, i], device)

    def row_start(stage):
        pl.when(has_right)(lambda: row_copy(stage, 0).start())
        pl.when(has_left)(lambda: row_copy(stage, 1).start())
        row_copy(stage, 2).start()

    def row_wait(stage):
        pl.when(has_left)(lambda: row_copy(stage, 0).wait_recv())
        pl.when(has_right)(lambda: row_copy(stage, 1).wait_recv())
        pl.when(inner)(lambda: row_copy(stage, 3).start())
        row_copy(stage, 2).wait_recv()
        pl.when(outer)(lambda: row_copy(stage, 3).wait_recv())

    def row_drain(stage):
        pl.when(has_right)(lambda: row_copy(stage, 0).wait_send())
        pl.when(has_left)(lambda: row_copy(stage, 1).wait_send())
        row_copy(stage, 2).wait_send()
        pl.when(inner)(lambda: row_copy(stage, 3).wait_send())

    top, low = pl.ds(0, half), pl.ds(half, half)

    def col_copy(stage, i):
        t, m, y, g = term.at[stage], mid.at[stage], relayed.at[stage], got.at[stage]
        src, dst, device = (
            (t.at[2, top], m.at[0], col_right), (t.at[2, low], m.at[1], col_left),
            (t.at[1, low], g.at[0, low], col_right), (t.at[3, top], g.at[1, top], col_left),
            (y.at[0], g.at[0, top], col_right), (y.at[1], g.at[1, low], col_left))[i]
        return remote(src, dst, col_send.at[stage, i], col_recv.at[stage, i], device)

    def share_copy(stage, i):
        held = shared.at[stage]
        src, dst, device = (
            (held.at[0, top], held.at[1, top], col_right),
            (held.at[0, low], held.at[3, low], col_left),
            (held.at[0, low], held.at[1, low], col_right),
            (held.at[0, top], held.at[3, top], col_left),
            (held.at[1, top], held.at[2, top], col_right),
            (held.at[3, low], held.at[2, low], col_left))[i]
        return remote(src, dst, share_send.at[stage, i], share_recv.at[stage, i], device)

    def share_start(stage, *which):
        for i in which:
            share_copy(stage, i).start()

    def share_forward(stage):
        for i in (0, 1):
            share_copy(stage, i).wait_recv()
            share_copy(stage, 4 + i).start()

    def share_wait(stage):
        for i in range(2, 6):
            share_copy(stage, i).wait_recv()

    def quarter(k):
        return pl.ds(pl.multiple_of(lax.rem(c + k, n_col) * node_rows, node_rows), node_rows)

    def weight_copy(k):
        device = {1: col_right, 2: col_across, 3: col_left}[k]
        return remote(w2.at[odd, :, quarter(k)], spread_w.at[odd, k - 1],
                      w_send.at[0, k - 1], w_recv.at[0, k - 1], device)

    def weight_forward(k):
        block = spread_w.at[odd, k - 1]
        return remote(block, block, w_send.at[1, k - 1], w_recv.at[1, k - 1], sibling)

    row_start(0)
    for copy in loads[7:]:
        copy.wait()
    for k in (2, 1, 3):
        weight_copy(k).start()
    for copy in mask_loads[:wide]:
        copy.wait()
    for p in range(wide):
        shared[p, 0] = (2 * mask_v[p]).astype(BF16)
    share_start(0, 0, 1)
    for copy in loads[1:5]:
        copy.wait()
    me = r * blocks - 2 * blocks
    local = [jnp.clip(cols_s[s] - me, 0, 5 * blocks - 1) for s in range(slots)]
    for s in range(slots):
        live = s < count_s[0]
        for b in range(blocks):
            here = jnp.logical_and(live, rows_s[s] == b)
            keep = jnp.where(here, 1.0, 0.0).astype(BF16)
            placed[pl.ds(b * BS, BS), pl.ds(s * BS, BS)] = adj_v[s] * keep
    degree = jnp.dot(placed[...], jnp.ones((slots * BS, 2 * BS), BF16),
                     preferred_element_type=F32)
    scale[...] = lax.rsqrt(degree)

    def aggregate(stage):
        tiles = jnp.concatenate([ext[stage][i] for i in local], axis=0)
        summed = jnp.dot(placed[...], tiles, preferred_element_type=F32)
        return summed * scale[...]

    def own_rows(stage):
        return jnp.concatenate([ext[stage][2 * blocks + b] for b in range(blocks)], axis=0)

    def product(left, weight, k):
        return jnp.dot(left, weight[:, quarter(k)], preferred_element_type=F32)

    def matmul(left, right):
        return jnp.dot(left, right, preferred_element_type=F32)

    def self_project(stage, w_self):
        mine = own_rows(stage)
        for k in range(n_col):
            self_term[stage, k] = product(mine, w_self, k)

    def spread(stage, share):
        for k, sent in ((2, (0, 1)), (1, (2,)), (3, (3,)), (0, ())):
            term[stage, k] = share(k).astype(BF16)
            for i in sent:
                col_copy(stage, i).start()

    def spread_terms(row_stage, col_stage, w_neigh):
        row_wait(row_stage)
        agg = aggregate(row_stage).astype(BF16)
        spread(col_stage, lambda k: self_term[row_stage, k] + product(agg, w_neigh, k))

    def relay(stage):
        for i, mine in ((0, term[stage, 1, top]), (1, term[stage, 3, low])):
            col_copy(stage, i).wait_recv()
            both = mine.astype(F32) + mid[stage, i].astype(F32)
            relayed[stage, i] = both.astype(BF16)
            col_copy(stage, 4 + i).start()

    def gathered(stage):
        for i in range(2, 6):
            col_copy(stage, i).wait_recv()
        return (term[stage, 0].astype(F32) + got[stage, 0].astype(F32)
                + got[stage, 1].astype(F32))

    loads[5].wait()
    self_project(0, ws1)
    loads[6].wait()
    spread_terms(0, 0, wn1)
    share_start(1, 0, 1)
    for copy in mask_loads[wide:]:
        copy.wait()
    relay(0)
    share_start(0, 2, 3)
    for k in (1, 3, 2):
        weight_copy(k).wait_recv()
        weight_forward(k).start()
    share_forward(0)
    hidden = jnp.maximum(gathered(0), 0.0).astype(BF16)
    doubled = (hidden + hidden).astype(F32)

    def send_rows(stage, value):
        for b in range(blocks):
            ext[stage][2 * blocks + b] = value[b * BS:(b + 1) * BS]
        row_start(stage)

    def send_dropped(p):
        send_rows(1 + p, (doubled * mask_v[p].astype(F32)).astype(BF16))

    send_dropped(wide)
    shared[wide, 0] = hidden
    share_start(wide, 0, 1, 2, 3)
    for p in narrow[1:]:
        send_dropped(p)
    for p in range(1, wide):
        share_start(p, 2, 3)
    for p in narrow:
        self_project(1 + p, w2.at[0])
    for stage in range(wide, 0, -1):
        share_forward(stage)
    for k in (1, 3, 2):
        weight_forward(k).wait_recv()

    def project_wide(p):
        share_wait(p)
        totals = [jnp.zeros((node_rows, node_rows), F32)] * 2
        for k in range(n_col):
            kept = (shared[wide, k].astype(F32) * shared[p, k].astype(F32)).astype(BF16)
            for m in range(2):
                block = spread_w[m, k - 1] if k else w2[m, :, quarter(0)]
                totals[m] = totals[m] + matmul(kept, block)
        self_wide[p] = totals[0]
        send_rows(1 + p, totals[1].astype(BF16))

    for i, p in enumerate(narrow):
        spread_terms(1 + p, 1 + i, w2.at[1])
        if i == 0:
            share_wait(wide)
        project_wide(i)
    for i, p in enumerate(narrow):
        relay(1 + i)
    for p in range(wide):
        row_wait(1 + p)
        out[p] = (self_wide[p] + aggregate(1 + p)).astype(BF16)
    for i, p in enumerate(narrow):
        out[p] = gathered(1 + i).astype(BF16)
    for stage in range(1 + passes):
        row_drain(stage)
    for i in range(6):
        for stage in range(1 + len(narrow)):
            col_copy(stage, i).wait_send()
        for stage in range(1 + wide):
            share_copy(stage, i).wait_send()
    for k in range(1, n_col):
        weight_copy(k).wait_send()
        weight_forward(k).wait_send()


def interleave(stacked, out):
    passes, rows, _ = stacked.shape
    step = 32
    for low in range(0, rows, step):
        part = stacked[:, low:low + step, :].astype(F32)
        out[low:low + step] = jnp.swapaxes(part, 0, 1).astype(BF16)


def solution(mesh):
    n_row, n_col = mesh.shape["row"], mesh.shape["col"]

    def on_device(features, masks, adj, adj_rows, adj_cols, adj_count, *weights):
        node_rows, width = features.shape
        blocks, slots, passes = node_rows // BS, adj_rows.shape[0], masks.shape[1]
        hidden = weights[0].shape[1]
        wide = passes // 2
        scatters = 1 + passes - wide
        dma = pltpu.SemaphoreType.DMA
        tile, halved = (node_rows, width), (node_rows // 2, width)
        ext = pltpu.VMEM((5 * blocks, BS, width), BF16)
        any_spec = pl.BlockSpec(memory_space=pl.ANY)
        vmem_spec = pl.BlockSpec(memory_space=pltpu.VMEM)
        stacked = pl.pallas_call(
            functools.partial(fused, n_row, n_col, passes, wide, blocks, slots),
            out_shape=pltpu.VMEM((passes,) + tile, BF16),
            in_specs=[any_spec] * 10,
            out_specs=vmem_spec,
            scratch_shapes=[
                pltpu.SMEM((slots,), jnp.int32), pltpu.SMEM((slots,), jnp.int32),
                pltpu.SMEM((1,), jnp.int32),
                pltpu.VMEM(adj.shape, BF16), pltpu.VMEM((node_rows, slots * BS), BF16),
                pltpu.VMEM(tile, F32),
                pltpu.VMEM((width, hidden), BF16), pltpu.VMEM((width, hidden), BF16),
                pltpu.VMEM((2, width, hidden), BF16),
                pltpu.VMEM((passes,) + tile, jnp.int32),
                pltpu.VMEM((1 + passes, n_col) + tile, F32),
                pltpu.VMEM((scatters, n_col) + tile, BF16),
                pltpu.VMEM((scatters, 2) + halved, BF16),
                pltpu.VMEM((scatters, 2) + halved, BF16),
                pltpu.VMEM((scatters, 2) + tile, BF16),
                pltpu.VMEM((2, n_col - 1) + tile, BF16),
                pltpu.VMEM((1 + wide, n_col) + tile, BF16),
                pltpu.VMEM((wide,) + tile, F32),
            ] + [ext] * (1 + passes) + [
                dma((9,)), dma((passes,)), dma((1 + passes, 4)), dma((1 + passes, 4)),
                dma((scatters, 6)), dma((scatters, 6)), dma((1 + wide, 6)),
                dma((1 + wide, 6)), dma((2, n_col - 1)), dma((2, n_col - 1)),
            ],
            compiler_params=pltpu.CompilerParams(
                collective_id=0, has_side_effects=True, vmem_limit_bytes=48 * 2**20),
        )(*[pltpu.with_memory_space_constraint(x, pltpu.HBM) if x.size > 1 else x for x in (
            features.reshape(blocks, BS, width), masks, adj, adj_rows, adj_cols, adj_count, *weights)])
        return pl.pallas_call(
            interleave,
            out_shape=jax.ShapeDtypeStruct((node_rows, passes, width), BF16),
            in_specs=[vmem_spec],
            out_specs=vmem_spec,
            compiler_params=pltpu.CompilerParams(vmem_limit_bytes=16 * 2**20),
        )(stacked)

    in_specs = (
        P("row", "col"), P("row", None, "col"), P("row", None, None), P("row"), P("row"),
        P("row"), P("col", None), P("col", None), P("col", None), P("col", None),
    )
    return jax.shard_map(on_device, mesh=mesh, in_specs=in_specs,
                         out_specs=P("row", None, "col"), check_vma=False)
```

```python
import functools

import jax
import jax.numpy as jnp
from jax import lax
from jax.experimental import pallas as pl
from jax.experimental.pallas import tpu as pltpu
from jax.sharding import PartitionSpec as P

BS = 128
LINE = 4
MESH = pl.DeviceIdType.MESH
BF16, F32 = jnp.bfloat16, jnp.float32


def fused(n_row, n_col, passes, wide, blocks, slots, *refs):
    (features, masks, adj, adj_rows, adj_cols, adj_count, w_self_one, w_neigh_one,
     w_self_two, w_neigh_two, out) = refs[:11]
    rest = list(refs[11:])
    rows_s, cols_s, count_s, adj_v, placed, scale, ws1, wn1, w2, mask_v = rest[:10]
    self_term, term, mid, relayed, got, spread_w, shared, self_wide = rest[10:18]
    ext = rest[18:19 + passes]
    (load_sem, row_send, far_recv, near_recv, col_send, col_recv, share_send, share_recv,
     w_send, w_recv) = rest[19 + passes:]

    r, c = lax.axis_index("row"), lax.axis_index("col")
    odd = lax.rem(r, 2)
    has_left, has_right = r >= 2, r < n_row - 2
    inner = jnp.where(odd == 0, has_right, has_left)
    outer = jnp.where(odd == 0, has_left, has_right)
    sibling = (r + 1 - 2 * odd, c)
    far_right, far_left = (lax.rem(r + 2, n_row), c), (lax.rem(r + n_row - 2, n_row), c)
    col_right, col_left = (r, lax.rem(c + 1, n_col)), (r, lax.rem(c + n_col - 1, n_col))
    narrow = range(wide, passes)
    row_parts = [2 if stage == 1 + wide else 1 for stage in range(1 + passes)]
    col_across = (r, lax.rem(c + 2, n_col))
    node_rows = blocks * BS
    piece, tall = node_rows // 4, node_rows // 2
    line = 2 * LINE
    spot = lax.rem(r // 2, LINE)

    barrier = pltpu.get_barrier_semaphore()

    def greet(device):
        pl.semaphore_signal(barrier, 1, device_id=device, device_id_type=MESH)

    pl.when(has_right)(lambda: greet(far_right))
    pl.when(has_left)(lambda: greet(far_left))
    def along_line(by):
        return (r - lax.rem(r, line) + lax.rem(r + 2 * by, line), c)

    for device in (sibling, col_right, col_left, col_across) + tuple(
            along_line(by) for by in range(1, LINE)):
        greet(device)

    loads = []
    own = ext[0].at[pl.ds(2 * blocks, blocks)]
    for i, src, dst in (
        (0, features, own), (1, adj, adj_v), (2, adj_rows, rows_s), (3, adj_cols, cols_s),
        (4, adj_count, count_s), (5, w_self_one, ws1), (6, w_neigh_one, wn1),
        (7, w_self_two, w2.at[0]), (7, w_neigh_two, w2.at[1]),
    ):
        loads.append(pltpu.make_async_copy(src, dst, load_sem.at[i]))
    mask_loads = [
        pltpu.make_async_copy(masks.at[:, p, :], mask_v.at[p], load_sem.at[8])
        for p in range(passes)
    ]

    def wait_for(ref, sem):
        pltpu.make_async_copy(ref, ref, sem).wait()

    for copy in loads + mask_loads:
        copy.start()
    loads[0].wait()
    pl.semaphore_wait(
        barrier, 3 + LINE + has_left.astype(jnp.int32) + has_right.astype(jnp.int32))

    def remote(src, dst, send, recv, device):
        return pltpu.make_async_remote_copy(
            src_ref=src, dst_ref=dst, send_sem=send, recv_sem=recv, device_id=device,
            device_id_type=MESH)

    def row_copy(stage, i, part):
        src, dst, device = (
            (2, 0, far_right), (2, 4, far_left), (2, 1 + 2 * odd, sibling),
            (4 - 4 * odd, 3 - 2 * odd, sibling))[i]
        size = blocks // row_parts[stage]
        pairs = [ext[stage].at[pl.ds(n * blocks + part * size, size)] for n in (src, dst)]
        recv = far_recv.at[stage, part] if i < 2 else near_recv.at[stage]
        return remote(*pairs, row_send.at[stage], recv, device)

    def row_start(stage, part):
        pl.when(has_right)(lambda: row_copy(stage, 0, part).start())
        pl.when(has_left)(lambda: row_copy(stage, 1, part).start())
        row_copy(stage, 2, part).start()

    def one_of(flag, stage, many, few, sem):
        pl.when(flag)(lambda: wait_for(ext[stage].at[pl.ds(0, many)], sem))
        pl.when(jnp.logical_not(flag))(lambda: wait_for(ext[stage].at[pl.ds(0, few)], sem))

    both = jnp.logical_and(has_left, has_right)

    def row_wait(stage):
        size = blocks // row_parts[stage]
        for part in range(row_parts[stage]):
            one_of(both, stage, 2 * size, size, far_recv.at[stage, part])
            pl.when(inner)(lambda: row_copy(stage, 3, part).start())
        one_of(outer, stage, 2 * blocks, blocks, near_recv.at[stage])

    def row_drain(stage):
        sent = row_send.at[stage]
        pl.when(both)(lambda: wait_for(ext[stage].at[pl.ds(0, 4 * blocks)], sent))

        @pl.when(jnp.logical_not(both))
        def _():
            one_of(inner, stage, 3 * blocks, 2 * blocks, sent)

    def rows(j):
        return pl.ds(j * piece, piece)

    def toward(j):
        return (col_right, col_left)[j % 2]

    def onward(j):
        return (1, 3)[j % 2]

    def col_copy(stage, i):
        t, g = term.at[stage], got.at[stage]
        j = i % 4
        if i < 4:
            src, dst, device = t.at[2, rows(j)], mid.at[stage, rows(j)], toward(j)
        elif i < 8:
            src, dst, device = relayed.at[stage, rows(j)], g.at[j % 2, rows(j)], toward(j)
        else:
            k = 4 - onward(j)
            src, dst, device = t.at[k, rows(j)], g.at[1 - j % 2, rows(j)], toward(j + 1)
        recv = col_recv.at[stage, 0 if i < 4 else 1, j // 2]
        return remote(src, dst, col_send.at[stage], recv, device)

    def share_copy(stage, i):
        held = shared.at[stage]
        j = i % 4
        if i < 4:
            src, dst, device = 0, onward(j), toward(j)
        elif i < 8:
            src, dst, device = 0, 4 - onward(j), toward(j + 1)
        else:
            src, dst, device = onward(j), 2, toward(j)
        return remote(held.at[src, rows(j)], held.at[dst, rows(j)], share_send.at[stage],
                      share_recv.at[stage, j // 2 if i < 4 else 2], device)

    def share_start(stage, *which):
        for i in which:
            share_copy(stage, i).start()

    def tall_rows(part):
        return pl.ds(part * tall, tall)

    def share_forward(stage):
        for part in (0, 1):
            wait_for(shared.at[stage, 1, tall_rows(part)], share_recv.at[stage, part])
            share_start(stage, 8 + 2 * part, 9 + 2 * part)

    def share_wait(stage):
        wait_for(shared.at[stage, pl.ds(1, 2)], share_recv.at[stage, 2])

    def quarter(k):
        return pl.ds(pl.multiple_of(lax.rem(c + k, n_col) * node_rows, node_rows), node_rows)

    part_rows = pl.ds(pl.multiple_of(spot * piece, piece), piece)

    def weight_copy(k):
        device = {1: col_right, 2: col_across, 3: col_left}[k]
        return remote(w2.at[odd, part_rows, quarter(k)], spread_w.at[odd, k - 1, part_rows],
                      w_send.at[0], w_recv.at[0], device)

    def line_copy(by):
        part = spread_w.at[odd, :, part_rows]
        return remote(part, part, w_send.at[1], w_recv.at[1], along_line(by))

    def weight_forward():
        blocks_held = spread_w.at[odd]
        return remote(blocks_held, blocks_held, w_send.at[2], w_recv.at[2], sibling)

    row_start(0, 0)
    wait_for(w2, load_sem.at[7])
    for k in (2, 1, 3):
        weight_copy(k).start()
    wait_for(mask_v, load_sem.at[8])
    for p in range(wide):
        shared[p, 0] = (2 * mask_v[p]).astype(BF16)
    share_start(0, 0, 1, 2, 3, 4, 5, 6, 7)
    share_start(1, 0, 1, 2, 3)
    for copy in loads[1:5]:
        copy.wait()
    me = r * blocks - 2 * blocks
    local = [jnp.clip(cols_s[s] - me, 0, 5 * blocks - 1) for s in range(slots)]
    for s in range(slots):
        live = s < count_s[0]
        for b in range(blocks):
            here = jnp.logical_and(live, rows_s[s] == b)
            keep = jnp.where(here, 1.0, 0.0).astype(BF16)
            placed[pl.ds(b * BS, BS), pl.ds(s * BS, BS)] = adj_v[s] * keep
    degree = jnp.dot(placed[...], jnp.ones((slots * BS, 2 * BS), BF16),
                     preferred_element_type=F32)
    scale[...] = lax.rsqrt(degree)

    def aggregate(stage):
        tiles = jnp.concatenate([ext[stage][i] for i in local], axis=0)
        summed = jnp.dot(placed[...], tiles, preferred_element_type=F32)
        return summed * scale[...]

    def own_rows(stage):
        return jnp.concatenate([ext[stage][2 * blocks + b] for b in range(blocks)], axis=0)

    def product(left, weight, k):
        return jnp.dot(left, weight[:, quarter(k)], preferred_element_type=F32)

    def matmul(left, right):
        return jnp.dot(left, right, preferred_element_type=F32)

    def self_project(stage, w_self):
        mine = own_rows(stage)
        for k in range(n_col):
            self_term[stage, k] = product(mine, w_self, k)

    def spread(stage, share):
        for k, sent in ((2, (0, 1, 2, 3)), (1, (9, 11)), (3, (8, 10)), (0, ())):
            term[stage, k] = share(k).astype(BF16)
            for i in sent:
                col_copy(stage, i).start()

    def spread_terms(row_stage, col_stage, w_neigh):
        row_wait(row_stage)
        agg = aggregate(row_stage).astype(BF16)
        spread(col_stage, lambda k: self_term[row_stage, k] + product(agg, w_neigh, k))

    def relay(stage, part):
        wait_for(mid.at[stage, tall_rows(part)], col_recv.at[stage, 0, part])
        for j in (2 * part, 2 * part + 1):
            both_terms = (term[stage, onward(j), rows(j)].astype(F32)
                          + mid[stage, rows(j)].astype(F32))
            relayed[stage, rows(j)] = both_terms.astype(BF16)
            col_copy(stage, 4 + j).start()

    def gathered(stage, part):
        wait_for(got.at[stage, :, tall_rows(part)], col_recv.at[stage, 1, part])
        here = tall_rows(part)
        return (term[stage, 0, here].astype(F32) + got[stage, 0, here].astype(F32)
                + got[stage, 1, here].astype(F32))

    loads[5].wait()
    self_project(0, ws1)
    loads[6].wait()
    spread_terms(0, 0, wn1)
    wait_for(spread_w.at[odd, :, part_rows], w_recv.at[0])
    for by in (2, 1, 3):
        line_copy(by).start()
    for part in (0, 1):
        relay(0, part)
    share_start(1, 4, 5, 6, 7)
    share_forward(0)

    def send_dropped(p, part):
        kept = (shared[wide, 0, tall_rows(part)].astype(F32)
                * (2 * mask_v[p, tall_rows(part)]).astype(F32)).astype(BF16)
        for b in range(blocks // 2):
            ext[1 + p][2 * blocks + part * (blocks // 2) + b] = kept[b * BS:(b + 1) * BS]

    for part in (0, 1):
        shared[wide, 0, tall_rows(part)] = jnp.maximum(gathered(0, part), 0.0).astype(BF16)
        share_start(wide, 2 * part, 2 * part + 1)
        send_dropped(wide, part)
        row_start(1 + wide, part)
    share_start(wide, 4, 5, 6, 7)
    for p in narrow[1:]:
        for part in (0, 1):
            send_dropped(p, part)
        row_start(1 + p, 0)
    share_forward(wide)
    share_forward(1)
    wait_for(spread_w.at[odd, :, pl.ds(0, 3 * piece)], w_recv.at[1])
    weight_forward().start()
    for p in narrow:
        self_project(1 + p, w2.at[0])

    def project_wide(p):
        share_wait(p)
        kept = [(shared[wide, k].astype(F32) * shared[p, k].astype(F32)).astype(BF16)
                for k in range(n_col)]

        def project(m):
            total = product(kept[0], w2.at[m], 0)
            for k in range(1, n_col):
                total = total + matmul(kept[k], spread_w[m, k - 1])
            return total

        value = project(1).astype(BF16)
        for b in range(blocks):
            ext[1 + p][2 * blocks + b] = value[b * BS:(b + 1) * BS]
        row_start(1 + p, 0)
        self_wide[p] = project(0)

    for i, p in enumerate(narrow):
        spread_terms(1 + p, 1 + i, w2.at[1])
        if i == 0:
            share_wait(wide)
            weight_forward().wait_recv()
        project_wide(i)
    for i, p in enumerate(narrow):
        for part in (0, 1):
            relay(1 + i, part)
    for p in range(wide):
        row_wait(1 + p)
        out[p] = (self_wide[p] + aggregate(1 + p)).astype(BF16)
    for i, p in enumerate(narrow):
        for part in (0, 1):
            out[p, tall_rows(part)] = gathered(1 + i, part).astype(BF16)
    for stage in range(1 + passes):
        row_drain(stage)
    for stage in range(1 + len(narrow)):
        wait_for(term.at[stage, pl.ds(0, 3)], col_send.at[stage])
    for stage in range(1 + wide):
        wait_for(shared.at[stage, pl.ds(0, 3)], share_send.at[stage])
    wait_for(spread_w.at[odd, :, part_rows], w_send.at[0])
    wait_for(spread_w.at[odd, :, pl.ds(0, 3 * piece)], w_send.at[1])
    wait_for(spread_w.at[odd], w_send.at[2])


def interleave(stacked, out):
    passes, rows, _ = stacked.shape
    step = 32
    for low in range(0, rows, step):
        part = stacked[:, low:low + step, :].astype(F32)
        out[low:low + step] = jnp.swapaxes(part, 0, 1).astype(BF16)


def solution(mesh):
    n_row, n_col = mesh.shape["row"], mesh.shape["col"]

    def on_device(features, masks, adj, adj_rows, adj_cols, adj_count, *weights):
        node_rows, width = features.shape
        blocks, slots, passes = node_rows // BS, adj_rows.shape[0], masks.shape[1]
        hidden = weights[0].shape[1]
        wide = passes // 2
        scatters = 1 + passes - wide
        dma = pltpu.SemaphoreType.DMA
        tile = (node_rows, width)
        ext = pltpu.VMEM((5 * blocks, BS, width), BF16)
        any_spec = pl.BlockSpec(memory_space=pl.ANY)
        vmem_spec = pl.BlockSpec(memory_space=pltpu.VMEM)
        stacked = pl.pallas_call(
            functools.partial(fused, n_row, n_col, passes, wide, blocks, slots),
            out_shape=pltpu.VMEM((passes,) + tile, BF16),
            in_specs=[any_spec] * 10,
            out_specs=vmem_spec,
            scratch_shapes=[
                pltpu.SMEM((slots,), jnp.int32), pltpu.SMEM((slots,), jnp.int32),
                pltpu.SMEM((1,), jnp.int32),
                pltpu.VMEM(adj.shape, BF16), pltpu.VMEM((node_rows, slots * BS), BF16),
                pltpu.VMEM(tile, F32),
                pltpu.VMEM((width, hidden), BF16), pltpu.VMEM((width, hidden), BF16),
                pltpu.VMEM((2, width, hidden), BF16),
                pltpu.VMEM((passes,) + tile, jnp.int32),
                pltpu.VMEM((1 + passes, n_col) + tile, F32),
                pltpu.VMEM((scatters, n_col) + tile, BF16),
                pltpu.VMEM((scatters,) + tile, BF16),
                pltpu.VMEM((scatters,) + tile, BF16),
                pltpu.VMEM((scatters, 2) + tile, BF16),
                pltpu.VMEM((2, n_col - 1) + tile, BF16),
                pltpu.VMEM((1 + wide, n_col) + tile, BF16),
                pltpu.VMEM((wide,) + tile, F32),
            ] + [ext] * (1 + passes) + [
                dma((9,)), dma((1 + passes,)), dma((1 + passes, 2)), dma((1 + passes,)),
                dma((scatters,)), dma((scatters, 2, 2)), dma((1 + wide,)),
                dma((1 + wide, 3)), dma((3,)), dma((3,)),
            ],
            compiler_params=pltpu.CompilerParams(
                collective_id=0, has_side_effects=True, vmem_limit_bytes=48 * 2**20),
        )(*[pltpu.with_memory_space_constraint(x, pltpu.HBM) if x.size > 1 else x for x in (
            features.reshape(blocks, BS, width), masks, adj, adj_rows, adj_cols, adj_count, *weights)])
        return pl.pallas_call(
            interleave,
            out_shape=jax.ShapeDtypeStruct((node_rows, passes, width), BF16),
            in_specs=[vmem_spec],
            out_specs=vmem_spec,
            compiler_params=pltpu.CompilerParams(vmem_limit_bytes=16 * 2**20),
        )(stacked)

    in_specs = (
        P("row", "col"), P("row", None, "col"), P("row", None, None), P("row"), P("row"),
        P("row"), P("col", None), P("col", None), P("col", None), P("col", None),
    )
    return jax.shard_map(on_device, mesh=mesh, in_specs=in_specs,
                         out_specs=P("row", None, "col"), check_vma=False)
```

```python
import functools

import jax
import jax.numpy as jnp
from jax import lax
from jax.experimental import pallas as pl
from jax.experimental.pallas import tpu as pltpu
from jax.sharding import PartitionSpec as P

BS = 128
LINE = 4
MESH = pl.DeviceIdType.MESH
BF16, F32 = jnp.bfloat16, jnp.float32


def fused(n_row, n_col, passes, wide, blocks, slots, *refs):
    (features, masks, adj, adj_rows, adj_cols, adj_count, w_self_one, w_neigh_one,
     w_self_two, w_neigh_two, out) = refs[:11]
    rest = list(refs[11:])
    rows_s, cols_s, count_s, adj_v, placed, scale, ws1, wn1, w2, mask_v = rest[:10]
    self_term, term, mid, relayed, got, spread_w, shared, self_wide = rest[10:18]
    ext = rest[18:19 + passes]
    (load_sem, row_send, far_recv, near_recv, col_send, col_recv, share_send, share_recv,
     w_send, w_recv) = rest[19 + passes:]

    r, c = lax.axis_index("row"), lax.axis_index("col")
    odd = lax.rem(r, 2)
    has_left, has_right = r >= 2, r < n_row - 2
    inner = jnp.where(odd == 0, has_right, has_left)
    outer = jnp.where(odd == 0, has_left, has_right)
    sibling = (r + 1 - 2 * odd, c)
    far_right, far_left = (lax.rem(r + 2, n_row), c), (lax.rem(r + n_row - 2, n_row), c)
    across = (r - 1 + 2 * odd, c)
    col_right, col_left = (r, lax.rem(c + 1, n_col)), (r, lax.rem(c + n_col - 1, n_col))
    narrow = range(wide, passes)
    mixed = [stage in (0, wide, 1 + wide) for stage in range(1 + passes)]
    col_across = (r, lax.rem(c + 2, n_col))
    node_rows = blocks * BS
    piece, tall = node_rows // 4, node_rows // 2
    line = 2 * LINE
    spot = lax.rem(r // 2, LINE)

    barrier = pltpu.get_barrier_semaphore()

    def greet(device):
        pl.semaphore_signal(barrier, 1, device_id=device, device_id_type=MESH)

    pl.when(has_right)(lambda: greet(far_right))
    pl.when(has_left)(lambda: greet(far_left))
    pl.when(outer)(lambda: greet(across))
    def along_line(by):
        return (r - lax.rem(r, line) + lax.rem(r + 2 * by, line), c)

    for device in (sibling, col_right, col_left, col_across) + tuple(
            along_line(by) for by in range(1, LINE)):
        greet(device)

    loads = []
    own = ext[0].at[pl.ds(2 * blocks, blocks)]
    for i, src, dst in (
        (0, features, own), (1, adj, adj_v), (2, adj_rows, rows_s), (3, adj_cols, cols_s),
        (4, adj_count, count_s), (5, w_self_one, ws1), (6, w_neigh_one, wn1),
        (7, w_self_two, w2.at[0]), (7, w_neigh_two, w2.at[1]),
    ):
        loads.append(pltpu.make_async_copy(src, dst, load_sem.at[i]))
    mask_loads = [
        pltpu.make_async_copy(masks.at[:, p, :], mask_v.at[p], load_sem.at[8])
        for p in range(passes)
    ]

    def wait_for(ref, sem):
        pltpu.make_async_copy(ref, ref, sem).wait()

    for copy in loads + mask_loads:
        copy.start()
    loads[0].wait()
    peers = sum(flag.astype(jnp.int32) for flag in (has_left, has_right, outer))
    pl.semaphore_wait(barrier, 3 + LINE + peers)

    def remote(src, dst, send, recv, device):
        return pltpu.make_async_remote_copy(
            src_ref=src, dst_ref=dst, send_sem=send, recv_sem=recv, device_id=device,
            device_id_type=MESH)

    def row_copy(stage, i, part):
        src, dst, device = (
            (2, 0, far_right), (2, 4, far_left), (2, 1 + 2 * odd, sibling),
            (4 - 4 * odd, 3 - 2 * odd, sibling), (2, 3 - 2 * odd, across))[i]
        size = blocks // 2 if mixed[stage] else blocks
        pairs = [ext[stage].at[pl.ds(n * blocks + part * size, size)] for n in (src, dst)]
        recv = far_recv.at[stage, part] if i < 2 else near_recv.at[stage]
        return remote(*pairs, row_send.at[stage], recv, device)

    def row_start(stage, part):
        pl.when(has_right)(lambda: row_copy(stage, 0, part).start())
        pl.when(has_left)(lambda: row_copy(stage, 1, part).start())
        if part:
            pl.when(outer)(lambda: row_copy(stage, 4, part).start())
        row_copy(stage, 2, part).start()

    def row_start_all(stage):
        for part in range(1 + mixed[stage]):
            row_start(stage, part)

    def one_of(flag, stage, many, few, sem):
        pl.when(flag)(lambda: wait_for(ext[stage].at[pl.ds(0, many)], sem))
        pl.when(jnp.logical_not(flag))(lambda: wait_for(ext[stage].at[pl.ds(0, few)], sem))

    both = jnp.logical_and(has_left, has_right)

    def row_wait(stage):
        size = blocks // 2 if mixed[stage] else blocks
        one_of(both, stage, 2 * size, size, far_recv.at[stage, 0])
        pl.when(inner)(lambda: row_copy(stage, 3, 0).start())
        if mixed[stage]:
            one_of(both, stage, 2 * size, size, far_recv.at[stage, 1])
        one_of(outer, stage, 2 * blocks, blocks, near_recv.at[stage])

    def row_drain(stage):
        sent = row_send.at[stage]
        half = blocks // 2
        if mixed[stage]:
            one_of(both, stage, 8 * half, 5 * half, sent)
            return
        pl.when(both)(lambda: wait_for(ext[stage].at[pl.ds(0, 8 * half)], sent))

        @pl.when(jnp.logical_not(both))
        def _():
            one_of(inner, stage, 6 * half, 4 * half, sent)

    def rows(j):
        return pl.ds(j * piece, piece)

    def toward(j):
        return (col_right, col_left)[j % 2]

    def onward(j):
        return (1, 3)[j % 2]

    def col_copy(stage, i):
        t, g = term.at[stage], got.at[stage]
        j = i % 4
        if i < 4:
            src, dst, device = t.at[2, rows(j)], mid.at[stage, rows(j)], toward(j)
        elif i < 8:
            src, dst, device = relayed.at[stage, rows(j)], g.at[j % 2, rows(j)], toward(j)
        else:
            k = 4 - onward(j)
            src, dst, device = t.at[k, rows(j)], g.at[1 - j % 2, rows(j)], toward(j + 1)
        recv = col_recv.at[stage, 0 if i < 4 else 1, j // 2]
        return remote(src, dst, col_send.at[stage], recv, device)

    def share_copy(stage, i):
        held = shared.at[stage]
        j = i % 4
        if i < 4:
            src, dst, device = 0, onward(j), toward(j)
        elif i < 8:
            src, dst, device = 0, 4 - onward(j), toward(j + 1)
        else:
            src, dst, device = onward(j), 2, toward(j)
        return remote(held.at[src, rows(j)], held.at[dst, rows(j)], share_send.at[stage],
                      share_recv.at[stage, j // 2 if i < 4 else 2], device)

    def share_start(stage, *which):
        for i in which:
            share_copy(stage, i).start()

    def tall_rows(part):
        return pl.ds(part * tall, tall)

    def share_forward(stage):
        for part in (0, 1):
            wait_for(shared.at[stage, 1, tall_rows(part)], share_recv.at[stage, part])
            share_start(stage, 8 + 2 * part, 9 + 2 * part)

    def share_wait(stage):
        wait_for(shared.at[stage, pl.ds(1, 2)], share_recv.at[stage, 2])

    def quarter(k):
        return pl.ds(pl.multiple_of(lax.rem(c + k, n_col) * node_rows, node_rows), node_rows)

    part_rows = pl.ds(pl.multiple_of(spot * piece, piece), piece)

    def weight_copy(k):
        device = {1: col_right, 2: col_across, 3: col_left}[k]
        return remote(w2.at[odd, part_rows, quarter(k)], spread_w.at[odd, k - 1, part_rows],
                      w_send.at[0], w_recv.at[0], device)

    def line_copy(by):
        part = spread_w.at[odd, :, part_rows]
        return remote(part, part, w_send.at[1], w_recv.at[1], along_line(by))

    def weight_forward():
        blocks_held = spread_w.at[odd]
        return remote(blocks_held, blocks_held, w_send.at[2], w_recv.at[2], sibling)

    row_start_all(0)
    wait_for(w2, load_sem.at[7])
    for k in (2, 1, 3):
        weight_copy(k).start()
    wait_for(mask_v, load_sem.at[8])
    for p in range(wide):
        shared[p, 0] = (2 * mask_v[p]).astype(BF16)
    share_start(0, 0, 1, 2, 3, 4, 5, 6, 7)
    share_start(1, 0, 1, 2, 3)
    for copy in loads[1:5]:
        copy.wait()
    me = r * blocks - 2 * blocks
    local = [jnp.clip(cols_s[s] - me, 0, 5 * blocks - 1) for s in range(slots)]
    for s in range(slots):
        live = s < count_s[0]
        for b in range(blocks):
            here = jnp.logical_and(live, rows_s[s] == b)
            keep = jnp.where(here, 1.0, 0.0).astype(BF16)
            placed[pl.ds(b * BS, BS), pl.ds(s * BS, BS)] = adj_v[s] * keep
    degree = jnp.dot(placed[...], jnp.ones((slots * BS, 2 * BS), BF16),
                     preferred_element_type=F32)
    scale[...] = lax.rsqrt(degree)

    def aggregate(stage):
        tiles = jnp.concatenate([ext[stage][i] for i in local], axis=0)
        summed = jnp.dot(placed[...], tiles, preferred_element_type=F32)
        return summed * scale[...]

    def own_rows(stage):
        return jnp.concatenate([ext[stage][2 * blocks + b] for b in range(blocks)], axis=0)

    def product(left, weight, k):
        return jnp.dot(left, weight[:, quarter(k)], preferred_element_type=F32)

    def matmul(left, right):
        return jnp.dot(left, right, preferred_element_type=F32)

    def self_project(stage, w_self):
        mine = own_rows(stage)
        for k in range(n_col):
            self_term[stage, k] = product(mine, w_self, k)

    def spread(stage, share):
        for k, sent in ((2, (0, 1, 2, 3)), (1, (9, 11)), (3, (8, 10)), (0, ())):
            term[stage, k] = share(k).astype(BF16)
            for i in sent:
                col_copy(stage, i).start()

    def spread_terms(row_stage, col_stage, w_neigh):
        row_wait(row_stage)
        agg = aggregate(row_stage).astype(BF16)
        spread(col_stage, lambda k: self_term[row_stage, k] + product(agg, w_neigh, k))

    def relay(stage, part):
        wait_for(mid.at[stage, tall_rows(part)], col_recv.at[stage, 0, part])
        for j in (2 * part, 2 * part + 1):
            both_terms = (term[stage, onward(j), rows(j)].astype(F32)
                          + mid[stage, rows(j)].astype(F32))
            relayed[stage, rows(j)] = both_terms.astype(BF16)
            col_copy(stage, 4 + j).start()

    def gathered(stage, part):
        wait_for(got.at[stage, :, tall_rows(part)], col_recv.at[stage, 1, part])
        here = tall_rows(part)
        return (term[stage, 0, here].astype(F32) + got[stage, 0, here].astype(F32)
                + got[stage, 1, here].astype(F32))

    loads[5].wait()
    self_project(0, ws1)
    loads[6].wait()
    spread_terms(0, 0, wn1)
    wait_for(spread_w.at[odd, :, part_rows], w_recv.at[0])
    for by in (2, 1, 3):
        line_copy(by).start()
    for part in (0, 1):
        relay(0, part)
    share_start(1, 4, 5, 6, 7)
    share_forward(0)

    def send_dropped(p, part):
        kept = (shared[wide, 0, tall_rows(part)].astype(F32)
                * (2 * mask_v[p, tall_rows(part)]).astype(F32)).astype(BF16)
        for b in range(blocks // 2):
            ext[1 + p][2 * blocks + part * (blocks // 2) + b] = kept[b * BS:(b + 1) * BS]

    for part in (0, 1):
        shared[wide, 0, tall_rows(part)] = jnp.maximum(gathered(0, part), 0.0).astype(BF16)
        share_start(wide, 2 * part, 2 * part + 1)
        send_dropped(wide, part)
        row_start(1 + wide, part)
    share_start(wide, 4, 5, 6, 7)
    for p in narrow[1:]:
        for part in (0, 1):
            send_dropped(p, part)
        row_start_all(1 + p)
    share_forward(wide)
    share_forward(1)
    wait_for(spread_w.at[odd, :, pl.ds(0, 3 * piece)], w_recv.at[1])
    weight_forward().start()
    for p in narrow:
        self_project(1 + p, w2.at[0])

    def project_wide(p):
        share_wait(p)
        kept = [(shared[wide, k].astype(F32) * shared[p, k].astype(F32)).astype(BF16)
                for k in range(n_col)]

        def project(m):
            total = product(kept[0], w2.at[m], 0)
            for k in range(1, n_col):
                total = total + matmul(kept[k], spread_w[m, k - 1])
            return total

        value = project(1).astype(BF16)
        for b in range(blocks):
            ext[1 + p][2 * blocks + b] = value[b * BS:(b + 1) * BS]
        row_start_all(1 + p)
        self_wide[p] = project(0)

    for i, p in enumerate(narrow):
        spread_terms(1 + p, 1 + i, w2.at[1])
        if i == 0:
            share_wait(wide)
            weight_forward().wait_recv()
        project_wide(i)
    for i, p in enumerate(narrow):
        for part in (0, 1):
            relay(1 + i, part)
    for p in range(wide):
        row_wait(1 + p)
        out[p] = (self_wide[p] + aggregate(1 + p)).astype(BF16)
    for i, p in enumerate(narrow):
        for part in (0, 1):
            out[p, tall_rows(part)] = gathered(1 + i, part).astype(BF16)
    for stage in range(1 + passes):
        row_drain(stage)
    for stage in range(1 + len(narrow)):
        wait_for(term.at[stage, pl.ds(0, 3)], col_send.at[stage])
    for stage in range(1 + wide):
        wait_for(shared.at[stage, pl.ds(0, 3)], share_send.at[stage])
    wait_for(spread_w.at[odd, :, part_rows], w_send.at[0])
    wait_for(spread_w.at[odd, :, pl.ds(0, 3 * piece)], w_send.at[1])
    wait_for(spread_w.at[odd], w_send.at[2])


def interleave(stacked, out):
    passes, rows, _ = stacked.shape
    step = 32
    for low in range(0, rows, step):
        part = stacked[:, low:low + step, :].astype(F32)
        out[low:low + step] = jnp.swapaxes(part, 0, 1).astype(BF16)


def solution(mesh):
    n_row, n_col = mesh.shape["row"], mesh.shape["col"]

    def on_device(features, masks, adj, adj_rows, adj_cols, adj_count, *weights):
        node_rows, width = features.shape
        blocks, slots, passes = node_rows // BS, adj_rows.shape[0], masks.shape[1]
        hidden = weights[0].shape[1]
        wide = passes // 2
        scatters = 1 + passes - wide
        dma = pltpu.SemaphoreType.DMA
        tile = (node_rows, width)
        ext = pltpu.VMEM((5 * blocks, BS, width), BF16)
        any_spec = pl.BlockSpec(memory_space=pl.ANY)
        vmem_spec = pl.BlockSpec(memory_space=pltpu.VMEM)
        stacked = pl.pallas_call(
            functools.partial(fused, n_row, n_col, passes, wide, blocks, slots),
            out_shape=pltpu.VMEM((passes,) + tile, BF16),
            in_specs=[any_spec] * 10,
            out_specs=vmem_spec,
            scratch_shapes=[
                pltpu.SMEM((slots,), jnp.int32), pltpu.SMEM((slots,), jnp.int32),
                pltpu.SMEM((1,), jnp.int32),
                pltpu.VMEM(adj.shape, BF16), pltpu.VMEM((node_rows, slots * BS), BF16),
                pltpu.VMEM(tile, F32),
                pltpu.VMEM((width, hidden), BF16), pltpu.VMEM((width, hidden), BF16),
                pltpu.VMEM((2, width, hidden), BF16),
                pltpu.VMEM((passes,) + tile, jnp.int32),
                pltpu.VMEM((1 + passes, n_col) + tile, F32),
                pltpu.VMEM((scatters, n_col) + tile, BF16),
                pltpu.VMEM((scatters,) + tile, BF16),
                pltpu.VMEM((scatters,) + tile, BF16),
                pltpu.VMEM((scatters, 2) + tile, BF16),
                pltpu.VMEM((2, n_col - 1) + tile, BF16),
                pltpu.VMEM((1 + wide, n_col) + tile, BF16),
                pltpu.VMEM((wide,) + tile, F32),
            ] + [ext] * (1 + passes) + [
                dma((9,)), dma((1 + passes,)), dma((1 + passes, 2)), dma((1 + passes,)),
                dma((scatters,)), dma((scatters, 2, 2)), dma((1 + wide,)),
                dma((1 + wide, 3)), dma((3,)), dma((3,)),
            ],
            compiler_params=pltpu.CompilerParams(
                collective_id=0, has_side_effects=True, vmem_limit_bytes=48 * 2**20),
        )(*[pltpu.with_memory_space_constraint(x, pltpu.HBM) if x.size > 1 else x for x in (
            features.reshape(blocks, BS, width), masks, adj, adj_rows, adj_cols, adj_count, *weights)])
        return pl.pallas_call(
            interleave,
            out_shape=jax.ShapeDtypeStruct((node_rows, passes, width), BF16),
            in_specs=[vmem_spec],
            out_specs=vmem_spec,
            compiler_params=pltpu.CompilerParams(vmem_limit_bytes=16 * 2**20),
        )(stacked)

    in_specs = (
        P("row", "col"), P("row", None, "col"), P("row", None, None), P("row"), P("row"),
        P("row"), P("col", None), P("col", None), P("col", None), P("col", None),
    )
    return jax.shard_map(on_device, mesh=mesh, in_specs=in_specs,
                         out_specs=P("row", None, "col"), check_vma=False)
```

```python
import functools

import jax
import jax.numpy as jnp
from jax import lax
from jax.experimental import pallas as pl
from jax.experimental.pallas import tpu as pltpu
from jax.sharding import PartitionSpec as P

BS = 128
LINE = 4
CHUNKS = 4
MESH = pl.DeviceIdType.MESH
BF16, F32 = jnp.bfloat16, jnp.float32


def fused(n_row, n_col, passes, wide, blocks, slots, *refs):
    (features, masks, adj, adj_rows, adj_cols, adj_count, w_self_one, w_neigh_one,
     w_self_two, w_neigh_two, out) = refs[:11]
    rest = list(refs[11:])
    rows_s, cols_s, count_s, adj_v, placed, scale, ws1, wn1, w2, mask_v = rest[:10]
    self_term, term, mid, relayed, got, spread_w, shared, self_wide = rest[10:18]
    ext = rest[18:19 + passes]
    (load_sem, row_send, far_recv, near_recv, sent, col_recv, share_recv,
     w_recv) = rest[19 + passes:]

    r, c = lax.axis_index("row"), lax.axis_index("col")
    odd = lax.rem(r, 2)
    has_left, has_right = r >= 2, r < n_row - 2
    inner = jnp.where(odd == 0, has_right, has_left)
    outer = jnp.where(odd == 0, has_left, has_right)
    sibling = (r + 1 - 2 * odd, c)
    far_right, far_left = (lax.rem(r + 2, n_row), c), (lax.rem(r + n_row - 2, n_row), c)
    across = (r - 1 + 2 * odd, c)
    col_right, col_left = (r, lax.rem(c + 1, n_col)), (r, lax.rem(c + n_col - 1, n_col))
    narrow = range(wide, passes)
    mixed = [stage in (0, wide, 1 + wide) for stage in range(1 + passes)]
    col_across = (r, lax.rem(c + 2, n_col))
    node_rows = blocks * BS
    piece, tall = node_rows // 4, node_rows // 2
    line = 2 * LINE
    spot, upper = lax.rem(r // 2, LINE), lax.rem(r // (2 * LINE), 2)
    paired = (r + line * (1 - 2 * upper), c)

    barrier = pltpu.get_barrier_semaphore()

    def greet(device):
        pl.semaphore_signal(barrier, 1, device_id=device, device_id_type=MESH)

    pl.when(has_right)(lambda: greet(far_right))
    pl.when(has_left)(lambda: greet(far_left))
    pl.when(outer)(lambda: greet(across))
    def along_line(by):
        return (r - lax.rem(r, line) + lax.rem(r + 2 * by, line), c)

    for device in (sibling, col_right, col_left, col_across, paired) + tuple(
            along_line(by) for by in range(1, LINE)):
        greet(device)

    loads = []
    own = ext[0].at[pl.ds(2 * blocks, blocks)]
    for i, src, dst in (
        (0, features, own), (5, adj, adj_v), (2, adj_rows, rows_s), (3, adj_cols, cols_s),
        (4, adj_count, count_s), (5, w_self_one, ws1), (5, w_neigh_one, wn1),
        (6, w_self_two, w2.at[0]), (6, w_neigh_two, w2.at[1]),
    ):
        loads.append(pltpu.make_async_copy(src, dst, load_sem.at[i]))
    mask_loads = [
        pltpu.make_async_copy(masks.at[:, p, :], mask_v.at[p], load_sem.at[7])
        for p in range(passes)
    ]

    def wait_for(ref, sem):
        pltpu.make_async_copy(ref, ref, sem).wait()

    for copy in loads + mask_loads:
        copy.start()
    loads[0].wait()
    peers = sum(flag.astype(jnp.int32) for flag in (has_left, has_right, outer))
    pl.semaphore_wait(barrier, 4 + LINE + peers)

    def remote(src, dst, send, recv, device):
        return pltpu.make_async_remote_copy(
            src_ref=src, dst_ref=dst, send_sem=send, recv_sem=recv, device_id=device,
            device_id_type=MESH)

    def row_copy(stage, i, part):
        src, dst, device = (
            (2, 0, far_right), (2, 4, far_left), (2, 1 + 2 * odd, sibling),
            (4 - 4 * odd, 3 - 2 * odd, sibling), (2, 3 - 2 * odd, across))[i]
        size = blocks // 2 if mixed[stage] else blocks
        pairs = [ext[stage].at[pl.ds(n * blocks + part * size, size)] for n in (src, dst)]
        recv = far_recv.at[stage, part] if i < 2 else near_recv.at[stage]
        return remote(*pairs, row_send.at[0 if mixed[stage] else 1], recv, device)

    def row_start(stage, part):
        pl.when(has_right)(lambda: row_copy(stage, 0, part).start())
        pl.when(has_left)(lambda: row_copy(stage, 1, part).start())
        if part:
            pl.when(outer)(lambda: row_copy(stage, 4, part).start())
        row_copy(stage, 2, part).start()

    def row_start_all(stage):
        for part in range(1 + mixed[stage]):
            row_start(stage, part)

    def one_of(flag, stage, many, few, sem):
        pl.when(flag)(lambda: wait_for(ext[stage].at[pl.ds(0, many)], sem))
        pl.when(jnp.logical_not(flag))(lambda: wait_for(ext[stage].at[pl.ds(0, few)], sem))

    both = jnp.logical_and(has_left, has_right)

    def row_wait(stage):
        size = blocks // 2 if mixed[stage] else blocks
        one_of(both, stage, 2 * size, size, far_recv.at[stage, 0])
        pl.when(inner)(lambda: row_copy(stage, 3, 0).start())
        if mixed[stage]:
            one_of(both, stage, 2 * size, size, far_recv.at[stage, 1])
        one_of(outer, stage, 2 * blocks, blocks, near_recv.at[stage])

    def row_drain():
        def drained(stages, blocks_each, sem):
            wait_for(self_term.at[pl.ds(0, stages), pl.ds(0, blocks_each), pl.ds(0, BS // 2)],
                     sem)

        some = sum(mixed)
        others = len(mixed) - some

        @pl.when(both)
        def _():
            whole = self_term.at[pl.ds(0, some), :, pl.ds(0, BS)]
            wait_for(whole, row_send.at[0])
            drained(2 * others, 4, row_send.at[1])

        @pl.when(jnp.logical_not(both))
        def _():
            drained(5, some, row_send.at[0])
            pl.when(inner)(lambda: drained(others + 1, 4, row_send.at[1]))
            pl.when(jnp.logical_not(inner))(lambda: drained(others, 4, row_send.at[1]))

    def rows(j):
        return pl.ds(j * piece, piece)

    def toward(j):
        return (col_right, col_left)[j % 2]

    def onward(j):
        return (1, 3)[j % 2]

    def col_copy(stage, i):
        t, g = term.at[stage], got.at[stage]
        j = i % 4
        if i < 4:
            src, dst, device = t.at[2, rows(j)], mid.at[stage, rows(j)], toward(j)
        elif i < 8:
            src, dst, device = relayed.at[stage, rows(j)], g.at[j % 2, rows(j)], toward(j)
        else:
            k = 4 - onward(j)
            src, dst, device = t.at[k, rows(j)], g.at[1 - j % 2, rows(j)], toward(j + 1)
        recv = col_recv.at[stage, 0 if i < 4 else 1, j // 2]
        return remote(src, dst, sent, recv, device)

    def share_copy(stage, i):
        held = shared.at[stage]
        j = i % 4
        if i < 4:
            src, dst, device = 0, onward(j), toward(j)
        elif i < 8:
            src, dst, device = 0, 4 - onward(j), toward(j + 1)
        else:
            src, dst, device = onward(j), 2, toward(j)
        return remote(held.at[src, rows(j)], held.at[dst, rows(j)], sent,
                      share_recv.at[stage, j // 2 if i < 4 else 2], device)

    def share_start(stage, *which):
        for i in which:
            share_copy(stage, i).start()

    def tall_rows(part):
        return pl.ds(part * tall, tall)

    def share_forward(stage):
        for part in (0, 1):
            wait_for(shared.at[stage, 1, tall_rows(part)], share_recv.at[stage, part])
            share_start(stage, 8 + 2 * part, 9 + 2 * part)

    def share_wait(stage):
        wait_for(shared.at[stage, pl.ds(1, 2)], share_recv.at[stage, 2])

    def quarter(k):
        return pl.ds(pl.multiple_of(lax.rem(c + k, n_col) * node_rows, node_rows), node_rows)

    part_rows = pl.ds(pl.multiple_of(spot * piece, piece), piece)

    slim = piece // 2
    slim_rows = pl.ds(pl.multiple_of(spot * piece + upper * slim, slim), slim)

    def weight_copy(k):
        device = {1: col_right, 2: col_across, 3: col_left}[k]
        return remote(w2.at[odd, slim_rows, quarter(k)], spread_w.at[odd, k - 1, slim_rows],
                      sent, w_recv.at[0], device)

    def pair_copy():
        part = spread_w.at[odd, :, slim_rows]
        return remote(part, part, sent, w_recv.at[3], paired)

    def line_copy(by):
        part = spread_w.at[odd, :, part_rows]
        return remote(part, part, sent, w_recv.at[1], along_line(by))

    def weight_forward():
        blocks_held = spread_w.at[odd]
        return remote(blocks_held, blocks_held, sent, w_recv.at[2], sibling)

    row_start_all(0)
    wait_for(w2, load_sem.at[6])
    for k in (2, 1, 3):
        weight_copy(k).start()
    wait_for(mask_v, load_sem.at[7])
    for p in range(wide):
        shared[p, 0] = (2 * mask_v[p]).astype(BF16)
    share_start(0, 0, 1, 2, 3, 4, 5, 6, 7)
    share_start(1, 0, 1, 2, 3, 4, 5, 6, 7)
    wait_for(self_term.at[:, 0], load_sem.at[5])
    for copy in loads[2:5]:
        copy.wait()
    me = r * blocks - 2 * blocks
    local = [jnp.clip(cols_s[s] - me, 0, 5 * blocks - 1) for s in range(slots)]
    for s in range(slots):
        live = s < count_s[0]
        for b in range(blocks):
            here = jnp.logical_and(live, rows_s[s] == b)
            keep = jnp.where(here, 1.0, 0.0).astype(BF16)
            placed[pl.ds(b * BS, BS), pl.ds(s * BS, BS)] = adj_v[s] * keep
    degree = jnp.dot(placed[...], jnp.ones((slots * BS, 2 * BS), BF16),
                     preferred_element_type=F32)
    scale[...] = lax.rsqrt(degree)

    def aggregate(stage):
        tiles = jnp.concatenate([ext[stage][i] for i in local], axis=0)
        summed = jnp.dot(placed[...], tiles, preferred_element_type=F32)
        return summed * scale[...]

    def own_rows(stage):
        return jnp.concatenate([ext[stage][2 * blocks + b] for b in range(blocks)], axis=0)

    def product(left, weight, k):
        return jnp.dot(left, weight[:, quarter(k)], preferred_element_type=F32)

    def matmul(left, right):
        return jnp.dot(left, right, preferred_element_type=F32)

    def self_project(stage, w_self):
        mine = own_rows(stage)
        for k in range(n_col):
            self_term[stage, k] = product(mine, w_self, k)

    def spread(stage, share):
        for k, sent in ((2, (0, 1, 2, 3)), (1, (9, 11)), (3, (8, 10)), (0, ())):
            term[stage, k] = share(k).astype(BF16)
            for i in sent:
                col_copy(stage, i).start()

    def spread_terms(row_stage, col_stage, w_neigh):
        row_wait(row_stage)
        agg = aggregate(row_stage).astype(BF16)
        spread(col_stage, lambda k: self_term[row_stage, k] + product(agg, w_neigh, k))

    def relay(stage, part):
        wait_for(mid.at[stage, tall_rows(part)], col_recv.at[stage, 0, part])
        for j in (2 * part, 2 * part + 1):
            both_terms = (term[stage, onward(j), rows(j)].astype(F32)
                          + mid[stage, rows(j)].astype(F32))
            relayed[stage, rows(j)] = both_terms.astype(BF16)
            col_copy(stage, 4 + j).start()

    def gathered(stage, part):
        wait_for(got.at[stage, :, tall_rows(part)], col_recv.at[stage, 1, part])
        here = tall_rows(part)
        return (term[stage, 0, here].astype(F32) + got[stage, 0, here].astype(F32)
                + got[stage, 1, here].astype(F32))

    self_project(0, ws1)
    wait_for(spread_w.at[odd, :, slim_rows], w_recv.at[0])
    pair_copy().start()
    spread_terms(0, 0, wn1)
    wait_for(spread_w.at[odd, :, slim_rows], w_recv.at[3])
    for by in (2, 1, 3):
        line_copy(by).start()
    for part in (0, 1):
        relay(0, part)
    share_forward(0)

    def send_dropped(p, part):
        kept = (shared[wide, 0, tall_rows(part)].astype(F32)
                * (2 * mask_v[p, tall_rows(part)]).astype(F32)).astype(BF16)
        for b in range(blocks // 2):
            ext[1 + p][2 * blocks + part * (blocks // 2) + b] = kept[b * BS:(b + 1) * BS]

    for part in (0, 1):
        shared[wide, 0, tall_rows(part)] = jnp.maximum(gathered(0, part), 0.0).astype(BF16)
        share_start(wide, 2 * part, 2 * part + 1)
        send_dropped(wide, part)
        row_start(1 + wide, part)
    share_start(wide, 4, 5, 6, 7)
    for p in narrow[1:]:
        for part in (0, 1):
            send_dropped(p, part)
        row_start_all(1 + p)
    share_forward(wide)
    share_forward(1)
    wait_for(spread_w.at[odd, :, pl.ds(0, 3 * piece)], w_recv.at[1])
    weight_forward().start()
    for p in narrow:
        self_project(1 + p, w2.at[0])

    def project_wide(p):
        share_wait(p)
        kept = [(shared[wide, k].astype(F32) * shared[p, k].astype(F32)).astype(BF16)
                for k in range(n_col)]

        def project(m):
            total = product(kept[0], w2.at[m], 0)
            for k in range(1, n_col):
                total = total + matmul(kept[k], spread_w[m, k - 1])
            return total

        value = project(1).astype(BF16)
        for b in range(blocks):
            ext[1 + p][2 * blocks + b] = value[b * BS:(b + 1) * BS]
        row_start_all(1 + p)
        self_wide[p] = project(0)

    for i, p in enumerate(narrow):
        spread_terms(1 + p, 1 + i, w2.at[1])
        if i == 0:
            share_wait(wide)
            weight_forward().wait_recv()
        project_wide(i)
    for i, p in enumerate(narrow):
        for part in (0, 1):
            relay(1 + i, part)
    for p in range(wide):
        row_wait(1 + p)
        out[p] = (self_wide[p] + aggregate(1 + p)).astype(BF16)
    for i, p in enumerate(narrow):
        for part in (0, 1):
            out[p, tall_rows(part)] = gathered(1 + i, part).astype(BF16)
    row_drain()
    wait_for(self_term.at[pl.ds(0, 3)], sent)


def interleave(stacked, out, held, sem):
    rows = stacked.shape[1]
    step, size = rows // 8, rows // CHUNKS
    copies = []
    for chunk in range(CHUNKS):
        for low in range(chunk * size, (chunk + 1) * size, step):
            part = stacked[:, low:low + step, :].astype(F32)
            held[low:low + step] = jnp.swapaxes(part, 0, 1).astype(BF16)
        span = pl.ds(chunk * size, size)
        copies.append(pltpu.make_async_copy(held.at[span], out.at[span], sem.at[chunk]))
        copies[-1].start()
    for copy in copies:
        copy.wait()


def solution(mesh):
    n_row, n_col = mesh.shape["row"], mesh.shape["col"]

    def on_device(features, masks, adj, adj_rows, adj_cols, adj_count, *weights):
        node_rows, width = features.shape
        blocks, slots, passes = node_rows // BS, adj_rows.shape[0], masks.shape[1]
        hidden = weights[0].shape[1]
        wide = passes // 2
        scatters = 1 + passes - wide
        dma = pltpu.SemaphoreType.DMA
        tile = (node_rows, width)
        ext = pltpu.VMEM((5 * blocks, BS, width), BF16)
        any_spec = pl.BlockSpec(memory_space=pl.ANY)
        vmem_spec = pl.BlockSpec(memory_space=pltpu.VMEM)
        stacked = pl.pallas_call(
            functools.partial(fused, n_row, n_col, passes, wide, blocks, slots),
            out_shape=pltpu.VMEM((passes,) + tile, BF16),
            in_specs=[any_spec] * 10,
            out_specs=vmem_spec,
            scratch_shapes=[
                pltpu.SMEM((slots,), jnp.int32), pltpu.SMEM((slots,), jnp.int32),
                pltpu.SMEM((1,), jnp.int32),
                pltpu.VMEM(adj.shape, BF16), pltpu.VMEM((node_rows, slots * BS), BF16),
                pltpu.VMEM(tile, F32),
                pltpu.VMEM((width, hidden), BF16), pltpu.VMEM((width, hidden), BF16),
                pltpu.VMEM((2, width, hidden), BF16),
                pltpu.VMEM((passes,) + tile, jnp.int32),
                pltpu.VMEM((1 + passes, n_col) + tile, F32),
                pltpu.VMEM((scatters, n_col) + tile, BF16),
                pltpu.VMEM((scatters,) + tile, BF16),
                pltpu.VMEM((scatters,) + tile, BF16),
                pltpu.VMEM((scatters, 2) + tile, BF16),
                pltpu.VMEM((2, n_col - 1) + tile, BF16),
                pltpu.VMEM((1 + wide, n_col) + tile, BF16),
                pltpu.VMEM((wide,) + tile, F32),
            ] + [ext] * (1 + passes) + [
                dma((8,)), dma((2,)), dma((1 + passes, 2)), dma((1 + passes,)), dma(()),
                dma((scatters, 2, 2)), dma((1 + wide, 3)), dma((4,)),
            ],
            compiler_params=pltpu.CompilerParams(
                collective_id=0, has_side_effects=True, vmem_limit_bytes=48 * 2**20),
        )(*[pltpu.with_memory_space_constraint(x, pltpu.HBM) if x.size > 1 else x for x in (
            features.reshape(blocks, BS, width), masks, adj, adj_rows, adj_cols, adj_count, *weights)])
        return pl.pallas_call(
            interleave,
            out_shape=jax.ShapeDtypeStruct((node_rows, passes, width), BF16),
            in_specs=[vmem_spec],
            out_specs=any_spec,
            scratch_shapes=[pltpu.VMEM((node_rows, passes, width), BF16), dma((CHUNKS,))],
            compiler_params=pltpu.CompilerParams(vmem_limit_bytes=16 * 2**20),
        )(stacked)

    in_specs = (
        P("row", "col"), P("row", None, "col"), P("row", None, None), P("row"), P("row"),
        P("row"), P("col", None), P("col", None), P("col", None), P("col", None),
    )
    return jax.shard_map(on_device, mesh=mesh, in_specs=in_specs,
                         out_specs=P("row", None, "col"), check_vma=False)
```

```python
import functools

import jax
import jax.numpy as jnp
from jax import lax
from jax.experimental import pallas as pl
from jax.experimental.pallas import tpu as pltpu
from jax.sharding import PartitionSpec as P

BS = 128
LINE = 4
CHUNKS = 4
MESH = pl.DeviceIdType.MESH
BF16, F32 = jnp.bfloat16, jnp.float32


def fused(n_row, n_col, passes, wide, blocks, slots, *refs):
    (features, masks, adj, adj_rows, adj_cols, adj_count, w_self_one, w_neigh_one,
     w_self_two, w_neigh_two, out) = refs[:11]
    rest = list(refs[11:])
    rows_s, cols_s, count_s, adj_v, placed, scale, ws1, wn1, w2, mask_v = rest[:10]
    self_term, term, mid, relayed, got, spread_w, shared, self_wide = rest[10:18]
    ext = rest[18:19 + passes]
    (load_sem, row_send, far_recv, near_recv, sent, col_recv, share_recv,
     w_recv) = rest[19 + passes:]

    r, c = lax.axis_index("row"), lax.axis_index("col")
    odd = lax.rem(r, 2)
    has_left, has_right = r >= 2, r < n_row - 2
    inner = jnp.where(odd == 0, has_right, has_left)
    outer = jnp.where(odd == 0, has_left, has_right)
    sibling = (r + 1 - 2 * odd, c)
    far_right, far_left = (lax.rem(r + 2, n_row), c), (lax.rem(r + n_row - 2, n_row), c)
    across = (r - 1 + 2 * odd, c)
    col_right, col_left = (r, lax.rem(c + 1, n_col)), (r, lax.rem(c + n_col - 1, n_col))
    narrow = range(wide, passes)
    scatters = 1 + len(narrow)
    mixed = [stage in (0, wide, 1 + wide) for stage in range(1 + passes)]
    col_across = (r, lax.rem(c + 2, n_col))
    node_rows = blocks * BS
    piece, tall = node_rows // 4, node_rows // 2
    line = 2 * LINE
    spot, upper = lax.rem(r // 2, LINE), lax.rem(r // (2 * LINE), 2)
    paired = (r + line * (1 - 2 * upper), c)

    barrier = pltpu.get_barrier_semaphore()

    def greet(device):
        pl.semaphore_signal(barrier, 1, device_id=device, device_id_type=MESH)

    pl.when(has_right)(lambda: greet(far_right))
    pl.when(has_left)(lambda: greet(far_left))
    pl.when(outer)(lambda: greet(across))
    def along_line(by):
        return (r - lax.rem(r, line) + lax.rem(r + 2 * by, line), c)

    for device in (sibling, col_right, col_left, col_across, paired) + tuple(
            along_line(by) for by in range(1, LINE)):
        greet(device)

    loads = []
    own = ext[0].at[pl.ds(2 * blocks, blocks)]
    for i, src, dst in (
        (0, features, own), (4, adj, adj_v), (1, adj_rows, rows_s), (2, adj_cols, cols_s),
        (3, adj_count, count_s), (4, w_self_one, ws1), (4, w_neigh_one, wn1),
        (5, w_self_two, w2.at[0]), (5, w_neigh_two, w2.at[1]),
    ):
        loads.append(pltpu.make_async_copy(src, dst, load_sem.at[i]))
    mask_loads = [
        pltpu.make_async_copy(masks.at[:, p, :], mask_v.at[p], load_sem.at[6])
        for p in range(passes)
    ]

    def wait_for(ref, sem):
        pltpu.make_async_copy(ref, ref, sem).wait()

    for copy in loads + mask_loads:
        copy.start()
    loads[0].wait()
    peers = sum(flag.astype(jnp.int32) for flag in (has_left, has_right, outer))
    pl.semaphore_wait(barrier, 4 + LINE + peers)

    def remote(src, dst, send, recv, device):
        return pltpu.make_async_remote_copy(
            src_ref=src, dst_ref=dst, send_sem=send, recv_sem=recv, device_id=device,
            device_id_type=MESH)

    def row_copy(stage, i, part):
        src, dst, device = (
            (2, 0, far_right), (2, 4, far_left), (2, 1 + 2 * odd, sibling),
            (4 - 4 * odd, 3 - 2 * odd, sibling), (2, 3 - 2 * odd, across))[i]
        size = blocks // 2 if mixed[stage] else blocks
        pairs = [ext[stage].at[pl.ds(n * blocks + part * size, size)] for n in (src, dst)]
        recv = far_recv.at[stage] if i < 2 and not part else near_recv.at[stage]
        return remote(*pairs, row_send.at[0 if mixed[stage] else 1], recv, device)

    def row_start(stage, part):
        pl.when(has_right)(lambda: row_copy(stage, 0, part).start())
        pl.when(has_left)(lambda: row_copy(stage, 1, part).start())
        if part:
            pl.when(outer)(lambda: row_copy(stage, 4, part).start())
        row_copy(stage, 2, part).start()

    def row_start_all(stage):
        for part in range(1 + mixed[stage]):
            row_start(stage, part)

    def one_of(flag, stage, many, few, sem):
        pl.when(flag)(lambda: wait_for(ext[stage].at[pl.ds(0, many)], sem))
        pl.when(jnp.logical_not(flag))(lambda: wait_for(ext[stage].at[pl.ds(0, few)], sem))

    both = jnp.logical_and(has_left, has_right)

    def row_wait(stage):
        size = blocks // 2 if mixed[stage] else blocks
        one_of(both, stage, 2 * size, size, far_recv.at[stage])
        pl.when(inner)(lambda: row_copy(stage, 3, 0).start())
        if not mixed[stage]:
            one_of(outer, stage, 2 * blocks, blocks, near_recv.at[stage])
            return
        pl.when(both)(lambda: wait_for(ext[stage].at[pl.ds(0, 6 * size)], near_recv.at[stage]))

        @pl.when(jnp.logical_not(both))
        def _():
            one_of(outer, stage, 5 * size, 3 * size, near_recv.at[stage])

    def row_drain():
        def drained(stages, blocks_each, sem):
            wait_for(self_term.at[pl.ds(0, stages), pl.ds(0, blocks_each), pl.ds(0, BS // 2)],
                     sem)

        some = sum(mixed)
        others = len(mixed) - some

        @pl.when(both)
        def _():
            whole = self_term.at[pl.ds(0, some), :, pl.ds(0, BS)]
            wait_for(whole, row_send.at[0])
            drained(2 * others, 4, row_send.at[1])

        @pl.when(jnp.logical_not(both))
        def _():
            drained(5, some, row_send.at[0])
            pl.when(inner)(lambda: drained(others + 1, 4, row_send.at[1]))
            pl.when(jnp.logical_not(inner))(lambda: drained(others, 4, row_send.at[1]))

    def rows(j):
        return pl.ds(j * piece, piece)

    def toward(j):
        return (col_right, col_left)[j % 2]

    def onward(j):
        return (1, 3)[j % 2]

    def first_recv(stage, part):
        return col_recv.at[3 * stage + part]

    def last_recv(stage, part):
        return col_recv.at[3 * stage + 2 if stage or not part else 3 * scatters]

    def col_copy(stage, i):
        t, g = term.at[stage], got.at[stage]
        j = i % 4
        if i < 4:
            src, dst, device = t.at[2, rows(j)], mid.at[stage, rows(j)], toward(j)
        elif i < 8:
            src, dst, device = relayed.at[stage, rows(j)], g.at[j % 2, rows(j)], toward(j)
        else:
            k = 4 - onward(j)
            src, dst, device = t.at[k, rows(j)], g.at[1 - j % 2, rows(j)], toward(j + 1)
        recv = first_recv(stage, j // 2) if i < 4 else last_recv(stage, j // 2)
        return remote(src, dst, sent, recv, device)

    def shared_recv(stage, n):
        if stage < wide:
            return share_recv.at[2 * stage + n // 2]
        return share_recv.at[2 * wide + n]

    def share_copy(stage, i):
        held = shared.at[stage]
        j = i % 4
        if i < 4:
            src, dst, device = 0, onward(j), toward(j)
        elif i < 8:
            src, dst, device = 0, 4 - onward(j), toward(j + 1)
        else:
            src, dst, device = onward(j), 2, toward(j)
        return remote(held.at[src, rows(j)], held.at[dst, rows(j)], sent,
                      shared_recv(stage, j // 2 if i < 4 else 2), device)

    def share_start(stage, *which):
        for i in which:
            share_copy(stage, i).start()

    def tall_rows(part):
        return pl.ds(part * tall, tall)

    def share_forward(stage):
        if stage < wide:
            wait_for(shared.at[stage, 1], shared_recv(stage, 0))
            share_start(stage, 8, 9, 10, 11)
            return
        for part in (0, 1):
            wait_for(shared.at[stage, 1, tall_rows(part)], shared_recv(stage, part))
            share_start(stage, 8 + 2 * part, 9 + 2 * part)

    def share_wait(stage):
        wait_for(shared.at[stage, pl.ds(1, 2)], shared_recv(stage, 2))

    def quarter(k):
        return pl.ds(pl.multiple_of(lax.rem(c + k, n_col) * node_rows, node_rows), node_rows)

    part_rows = pl.ds(pl.multiple_of(spot * piece, piece), piece)

    slim = piece // 2
    slim_rows = pl.ds(pl.multiple_of(spot * piece + upper * slim, slim), slim)

    def weight_copy(k):
        device = {1: col_right, 2: col_across, 3: col_left}[k]
        return remote(w2.at[odd, slim_rows, quarter(k)], spread_w.at[odd, k - 1, slim_rows],
                      sent, w_recv.at[0], device)

    def pair_copy():
        part = spread_w.at[odd, :, slim_rows]
        return remote(part, part, sent, w_recv.at[3], paired)

    def line_copy(by):
        part = spread_w.at[odd, :, part_rows]
        return remote(part, part, sent, w_recv.at[1], along_line(by))

    def weight_forward():
        blocks_held = spread_w.at[odd]
        return remote(blocks_held, blocks_held, sent, w_recv.at[2], sibling)

    row_start_all(0)
    wait_for(w2, load_sem.at[5])
    for k in (2, 1, 3):
        weight_copy(k).start()
    wait_for(mask_v, load_sem.at[6])
    for p in range(wide):
        shared[p, 0] = (2 * mask_v[p]).astype(BF16)
    share_start(0, 0, 1, 2, 3, 4, 5, 6, 7)
    share_start(1, 0, 1, 2, 3, 4, 5, 6, 7)
    wait_for(self_term.at[:, 0], load_sem.at[4])
    for copy in loads[2:5]:
        copy.wait()
    me = r * blocks - 2 * blocks
    local = [jnp.clip(cols_s[s] - me, 0, 5 * blocks - 1) for s in range(slots)]
    for s in range(slots):
        live = s < count_s[0]
        for b in range(blocks):
            here = jnp.logical_and(live, rows_s[s] == b)
            keep = jnp.where(here, 1.0, 0.0).astype(BF16)
            placed[pl.ds(b * BS, BS), pl.ds(s * BS, BS)] = adj_v[s] * keep
    degree = jnp.dot(placed[...], jnp.ones((slots * BS, 2 * BS), BF16),
                     preferred_element_type=F32)
    scale[...] = lax.rsqrt(degree)

    def aggregate(stage):
        tiles = jnp.concatenate([ext[stage][i] for i in local], axis=0)
        summed = jnp.dot(placed[...], tiles, preferred_element_type=F32)
        return summed * scale[...]

    def own_rows(stage):
        return jnp.concatenate([ext[stage][2 * blocks + b] for b in range(blocks)], axis=0)

    def product(left, weight, k):
        return jnp.dot(left, weight[:, quarter(k)], preferred_element_type=F32)

    def matmul(left, right):
        return jnp.dot(left, right, preferred_element_type=F32)

    def self_project(stage, w_self):
        mine = own_rows(stage)
        for k in range(n_col):
            self_term[stage, k] = product(mine, w_self, k)

    def spread(stage, share):
        for k, sent in ((2, (0, 1, 2, 3)), (1, (9, 11)), (3, (8, 10)), (0, ())):
            term[stage, k] = share(k).astype(BF16)
            for i in sent:
                col_copy(stage, i).start()

    def spread_terms(row_stage, col_stage, w_neigh):
        row_wait(row_stage)
        agg = aggregate(row_stage).astype(BF16)
        spread(col_stage, lambda k: self_term[row_stage, k] + product(agg, w_neigh, k))

    def relay(stage, part):
        wait_for(mid.at[stage, tall_rows(part)], first_recv(stage, part))
        for j in (2 * part, 2 * part + 1):
            both_terms = (term[stage, onward(j), rows(j)].astype(F32)
                          + mid[stage, rows(j)].astype(F32))
            relayed[stage, rows(j)] = both_terms.astype(BF16)
            col_copy(stage, 4 + j).start()

    def gathered(stage, part):
        if stage == 0:
            wait_for(got.at[stage, :, tall_rows(part)], last_recv(stage, part))
        elif part == 0:
            wait_for(got.at[stage], last_recv(stage, part))
        here = tall_rows(part)
        return (term[stage, 0, here].astype(F32) + got[stage, 0, here].astype(F32)
                + got[stage, 1, here].astype(F32))

    self_project(0, ws1)
    wait_for(spread_w.at[odd, :, slim_rows], w_recv.at[0])
    pair_copy().start()
    spread_terms(0, 0, wn1)
    wait_for(spread_w.at[odd, :, slim_rows], w_recv.at[3])
    for by in (2, 1, 3):
        line_copy(by).start()
    for part in (0, 1):
        relay(0, part)
    share_forward(0)

    def send_dropped(p, part):
        kept = (shared[wide, 0, tall_rows(part)].astype(F32)
                * (2 * mask_v[p, tall_rows(part)]).astype(F32)).astype(BF16)
        for b in range(blocks // 2):
            ext[1 + p][2 * blocks + part * (blocks // 2) + b] = kept[b * BS:(b + 1) * BS]

    for part in (0, 1):
        shared[wide, 0, tall_rows(part)] = jnp.maximum(gathered(0, part), 0.0).astype(BF16)
        share_start(wide, 2 * part, 2 * part + 1)
        send_dropped(wide, part)
        row_start(1 + wide, part)
    share_start(wide, 4, 5, 6, 7)
    for p in narrow[1:]:
        for part in (0, 1):
            send_dropped(p, part)
        row_start_all(1 + p)
    share_forward(wide)
    share_forward(1)
    wait_for(spread_w.at[odd, :, pl.ds(0, 3 * piece)], w_recv.at[1])
    weight_forward().start()
    for p in narrow:
        self_project(1 + p, w2.at[0])

    def project_wide(p):
        share_wait(p)
        kept = [(shared[wide, k].astype(F32) * shared[p, k].astype(F32)).astype(BF16)
                for k in range(n_col)]

        def project(m):
            total = product(kept[0], w2.at[m], 0)
            for k in range(1, n_col):
                total = total + matmul(kept[k], spread_w[m, k - 1])
            return total

        value = project(1).astype(BF16)
        for b in range(blocks):
            ext[1 + p][2 * blocks + b] = value[b * BS:(b + 1) * BS]
        row_start_all(1 + p)
        self_wide[p] = project(0)

    for i, p in enumerate(narrow):
        spread_terms(1 + p, 1 + i, w2.at[1])
        if i == 0:
            share_wait(wide)
            weight_forward().wait_recv()
        project_wide(i)
    for i, p in enumerate(narrow):
        for part in (0, 1):
            relay(1 + i, part)
    for p in range(wide):
        row_wait(1 + p)
        out[p] = (self_wide[p] + aggregate(1 + p)).astype(BF16)
    for i, p in enumerate(narrow):
        for part in (0, 1):
            out[p, tall_rows(part)] = gathered(1 + i, part).astype(BF16)
    row_drain()
    wait_for(self_term.at[pl.ds(0, 3)], sent)


def interleave(stacked, out, held, sem):
    rows = stacked.shape[1]
    step, size = rows // 8, rows // CHUNKS
    copies = []
    for chunk in range(CHUNKS):
        for low in range(chunk * size, (chunk + 1) * size, step):
            part = stacked[:, low:low + step, :].astype(F32)
            held[low:low + step] = jnp.swapaxes(part, 0, 1).astype(BF16)
        span = pl.ds(chunk * size, size)
        copies.append(pltpu.make_async_copy(held.at[span], out.at[span], sem.at[chunk]))
        copies[-1].start()
    for copy in copies:
        copy.wait()


def solution(mesh):
    n_row, n_col = mesh.shape["row"], mesh.shape["col"]

    def on_device(features, masks, adj, adj_rows, adj_cols, adj_count, *weights):
        node_rows, width = features.shape
        blocks, slots, passes = node_rows // BS, adj_rows.shape[0], masks.shape[1]
        hidden = weights[0].shape[1]
        wide = passes // 2
        scatters = 1 + passes - wide
        dma = pltpu.SemaphoreType.DMA
        tile = (node_rows, width)
        ext = pltpu.VMEM((5 * blocks, BS, width), BF16)
        any_spec = pl.BlockSpec(memory_space=pl.ANY)
        vmem_spec = pl.BlockSpec(memory_space=pltpu.VMEM)
        stacked = pl.pallas_call(
            functools.partial(fused, n_row, n_col, passes, wide, blocks, slots),
            out_shape=pltpu.VMEM((passes,) + tile, BF16),
            in_specs=[any_spec] * 10,
            out_specs=vmem_spec,
            scratch_shapes=[
                pltpu.SMEM((slots,), jnp.int32), pltpu.SMEM((slots,), jnp.int32),
                pltpu.SMEM((1,), jnp.int32),
                pltpu.VMEM(adj.shape, BF16), pltpu.VMEM((node_rows, slots * BS), BF16),
                pltpu.VMEM(tile, F32),
                pltpu.VMEM((width, hidden), BF16), pltpu.VMEM((width, hidden), BF16),
                pltpu.VMEM((2, width, hidden), BF16),
                pltpu.VMEM((passes,) + tile, jnp.int32),
                pltpu.VMEM((1 + passes, n_col) + tile, F32),
                pltpu.VMEM((scatters, n_col) + tile, BF16),
                pltpu.VMEM((scatters,) + tile, BF16),
                pltpu.VMEM((scatters,) + tile, BF16),
                pltpu.VMEM((scatters, 2) + tile, BF16),
                pltpu.VMEM((2, n_col - 1) + tile, BF16),
                pltpu.VMEM((1 + wide, n_col) + tile, BF16),
                pltpu.VMEM((wide,) + tile, F32),
            ] + [ext] * (1 + passes) + [
                dma((7,)), dma((2,)), dma((1 + passes,)), dma((1 + passes,)), dma(()),
                dma((3 * scatters + 1,)), dma((2 * wide + 3,)), dma((4,)),
            ],
            compiler_params=pltpu.CompilerParams(
                collective_id=0, has_side_effects=True, vmem_limit_bytes=48 * 2**20),
        )(*[pltpu.with_memory_space_constraint(x, pltpu.HBM) if x.size > 1 else x for x in (
            features.reshape(blocks, BS, width), masks, adj, adj_rows, adj_cols, adj_count, *weights)])
        return pl.pallas_call(
            interleave,
            out_shape=jax.ShapeDtypeStruct((node_rows, passes, width), BF16),
            in_specs=[vmem_spec],
            out_specs=any_spec,
            scratch_shapes=[pltpu.VMEM((node_rows, passes, width), BF16), dma((CHUNKS,))],
            compiler_params=pltpu.CompilerParams(vmem_limit_bytes=16 * 2**20),
        )(stacked)

    in_specs = (
        P("row", "col"), P("row", None, "col"), P("row", None, None), P("row"), P("row"),
        P("row"), P("col", None), P("col", None), P("col", None), P("col", None),
    )
    return jax.shard_map(on_device, mesh=mesh, in_specs=in_specs,
                         out_specs=P("row", None, "col"), check_vma=False)
```

```python
import functools

import jax
import jax.numpy as jnp
from jax import lax
from jax.experimental import pallas as pl
from jax.experimental.pallas import tpu as pltpu
from jax.sharding import PartitionSpec as P

BS = 128
LINE = 4
CHUNKS = 4
MESH = pl.DeviceIdType.MESH
BF16, F32 = jnp.bfloat16, jnp.float32


def fused(n_row, n_col, passes, wide, blocks, slots, *refs):
    (features, masks, adj, adj_rows, adj_cols, adj_count, w_self_one, w_neigh_one,
     w_self_two, w_neigh_two, out) = refs[:11]
    rest = list(refs[11:])
    rows_s, cols_s, count_s, adj_v, placed, scale, ws1, wn1, w2, mask_v = rest[:10]
    self_term, term, mid, relayed, got, spread_w, shared, self_wide = rest[10:18]
    ext = rest[18:19 + passes]
    (load_sem, row_send, far_recv, near_recv, sent, col_recv, share_recv,
     w_recv) = rest[19 + passes:]

    r, c = lax.axis_index("row"), lax.axis_index("col")
    odd = lax.rem(r, 2)
    has_left, has_right = r >= 2, r < n_row - 2
    inner = jnp.where(odd == 0, has_right, has_left)
    outer = jnp.where(odd == 0, has_left, has_right)
    sibling = (r + 1 - 2 * odd, c)
    far_right, far_left = (lax.rem(r + 2, n_row), c), (lax.rem(r + n_row - 2, n_row), c)
    across = (r - 1 + 2 * odd, c)
    col_right, col_left = (r, lax.rem(c + 1, n_col)), (r, lax.rem(c + n_col - 1, n_col))
    narrow = range(wide, passes)
    scatters = 1 + len(narrow)
    mixed = [stage in (0, wide, 1 + wide) for stage in range(1 + passes)]
    col_across = (r, lax.rem(c + 2, n_col))
    node_rows = blocks * BS
    piece, tall = node_rows // 4, node_rows // 2
    line = 2 * LINE
    spot, upper = lax.rem(r // 2, LINE), lax.rem(r // (2 * LINE), 2)
    paired = (r + line * (1 - 2 * upper), c)

    barrier = pltpu.get_barrier_semaphore()

    def greet(device):
        pl.semaphore_signal(barrier, 1, device_id=device, device_id_type=MESH)

    for device in (col_right, col_left, col_across):
        greet(device)
    pl.when(has_right)(lambda: greet(far_right))
    pl.when(has_left)(lambda: greet(far_left))
    pl.when(outer)(lambda: greet(across))
    def along_line(by):
        return (r - lax.rem(r, line) + lax.rem(r + 2 * by, line), c)

    for device in (sibling, paired) + tuple(
            along_line(by) for by in range(1, LINE)):
        greet(device)

    loads = []
    own = ext[0].at[pl.ds(2 * blocks, blocks)]
    for i, src, dst in (
        (0, features, own), (4, adj, adj_v), (1, adj_rows, rows_s), (2, adj_cols, cols_s),
        (3, adj_count, count_s), (4, w_self_one, ws1), (4, w_neigh_one, wn1),
        (5, w_self_two, w2.at[0]), (5, w_neigh_two, w2.at[1]),
    ):
        loads.append(pltpu.make_async_copy(src, dst, load_sem.at[i]))
    mask_loads = [
        pltpu.make_async_copy(masks.at[:, p, :], mask_v.at[p], load_sem.at[6])
        for p in range(passes)
    ]

    def wait_for(ref, sem):
        pltpu.make_async_copy(ref, ref, sem).wait()

    for copy in loads[:1] + loads[7:] + mask_loads + loads[1:7]:
        copy.start()
    loads[0].wait()
    peers = sum(flag.astype(jnp.int32) for flag in (has_left, has_right, outer))
    pl.semaphore_wait(barrier, 4 + LINE + peers)

    def remote(src, dst, send, recv, device):
        return pltpu.make_async_remote_copy(
            src_ref=src, dst_ref=dst, send_sem=send, recv_sem=recv, device_id=device,
            device_id_type=MESH)

    def row_copy(stage, i, part):
        src, dst, device = (
            (2, 0, far_right), (2, 4, far_left), (2, 1 + 2 * odd, sibling),
            (4 - 4 * odd, 3 - 2 * odd, sibling), (2, 3 - 2 * odd, across))[i]
        size = blocks // 2 if mixed[stage] else blocks
        pairs = [ext[stage].at[pl.ds(n * blocks + part * size, size)] for n in (src, dst)]
        recv = far_recv.at[stage] if i < 2 and not part else near_recv.at[stage]
        return remote(*pairs, row_send.at[0 if mixed[stage] else 1], recv, device)

    def row_start(stage, part):
        pl.when(has_right)(lambda: row_copy(stage, 0, part).start())
        pl.when(has_left)(lambda: row_copy(stage, 1, part).start())
        if part:
            pl.when(outer)(lambda: row_copy(stage, 4, part).start())
        row_copy(stage, 2, part).start()

    def row_start_all(stage):
        for part in range(1 + mixed[stage]):
            row_start(stage, part)

    def one_of(flag, stage, many, few, sem):
        pl.when(flag)(lambda: wait_for(ext[stage].at[pl.ds(0, many)], sem))
        pl.when(jnp.logical_not(flag))(lambda: wait_for(ext[stage].at[pl.ds(0, few)], sem))

    both = jnp.logical_and(has_left, has_right)

    def row_wait(stage):
        size = blocks // 2 if mixed[stage] else blocks
        one_of(both, stage, 2 * size, size, far_recv.at[stage])
        pl.when(inner)(lambda: row_copy(stage, 3, 0).start())
        if not mixed[stage]:
            one_of(outer, stage, 2 * blocks, blocks, near_recv.at[stage])
            return
        pl.when(both)(lambda: wait_for(ext[stage].at[pl.ds(0, 6 * size)], near_recv.at[stage]))

        @pl.when(jnp.logical_not(both))
        def _():
            one_of(outer, stage, 5 * size, 3 * size, near_recv.at[stage])

    def row_drain():
        def drained(stages, blocks_each, sem):
            wait_for(self_term.at[pl.ds(0, stages), pl.ds(0, blocks_each), pl.ds(0, BS // 2)],
                     sem)

        some = sum(mixed)
        others = len(mixed) - some

        @pl.when(both)
        def _():
            whole = self_term.at[pl.ds(0, some), :, pl.ds(0, BS)]
            wait_for(whole, row_send.at[0])
            drained(2 * others, 4, row_send.at[1])

        @pl.when(jnp.logical_not(both))
        def _():
            drained(5, some, row_send.at[0])
            pl.when(inner)(lambda: drained(others + 1, 4, row_send.at[1]))
            pl.when(jnp.logical_not(inner))(lambda: drained(others, 4, row_send.at[1]))

    def rows(j):
        return pl.ds(j * piece, piece)

    def toward(j):
        return (col_right, col_left)[j % 2]

    def onward(j):
        return (1, 3)[j % 2]

    def first_recv(stage, part):
        return col_recv.at[3 * stage + part]

    def last_recv(stage, part):
        return col_recv.at[3 * stage + 2 if stage or not part else 3 * scatters]

    def col_copy(stage, i):
        t, g = term.at[stage], got.at[stage]
        j = i % 4
        if i < 4:
            src, dst, device = t.at[2, rows(j)], mid.at[stage, rows(j)], toward(j)
        elif i < 8:
            src, dst, device = relayed.at[stage, rows(j)], g.at[j % 2, rows(j)], toward(j)
        else:
            k = 4 - onward(j)
            src, dst, device = t.at[k, rows(j)], g.at[1 - j % 2, rows(j)], toward(j + 1)
        recv = first_recv(stage, j // 2) if i < 4 else last_recv(stage, j // 2)
        return remote(src, dst, sent, recv, device)

    def shared_recv(stage, n):
        if stage < wide:
            return share_recv.at[2 * stage + n // 2]
        return share_recv.at[2 * wide + n]

    def share_copy(stage, i):
        held = shared.at[stage]
        j = i % 4
        if i < 4:
            src, dst, device = 0, onward(j), toward(j)
        elif i < 8:
            src, dst, device = 0, 4 - onward(j), toward(j + 1)
        else:
            src, dst, device = onward(j), 2, toward(j)
        return remote(held.at[src, rows(j)], held.at[dst, rows(j)], sent,
                      shared_recv(stage, j // 2 if i < 4 else 2), device)

    def share_start(stage, *which):
        for i in which:
            share_copy(stage, i).start()

    def tall_rows(part):
        return pl.ds(part * tall, tall)

    def share_forward(stage):
        if stage < wide:
            wait_for(shared.at[stage, 1], shared_recv(stage, 0))
            share_start(stage, 8, 9, 10, 11)
            return
        for part in (0, 1):
            wait_for(shared.at[stage, 1, tall_rows(part)], shared_recv(stage, part))
            share_start(stage, 8 + 2 * part, 9 + 2 * part)

    def share_wait(stage):
        wait_for(shared.at[stage, pl.ds(1, 2)], shared_recv(stage, 2))

    def quarter(k):
        return pl.ds(pl.multiple_of(lax.rem(c + k, n_col) * node_rows, node_rows), node_rows)

    part_rows = pl.ds(pl.multiple_of(spot * piece, piece), piece)

    slim = piece // 2
    slim_rows = pl.ds(pl.multiple_of(spot * piece + upper * slim, slim), slim)

    def weight_copy(k):
        device = {1: col_right, 2: col_across, 3: col_left}[k]
        return remote(w2.at[odd, slim_rows, quarter(k)], spread_w.at[odd, k - 1, slim_rows],
                      sent, w_recv.at[0], device)

    def pair_copy():
        part = spread_w.at[odd, :, slim_rows]
        return remote(part, part, sent, w_recv.at[3], paired)

    def line_copy(by):
        part = spread_w.at[odd, :, part_rows]
        return remote(part, part, sent, w_recv.at[1], along_line(by))

    def weight_forward():
        blocks_held = spread_w.at[odd]
        return remote(blocks_held, blocks_held, sent, w_recv.at[2], sibling)

    row_start_all(0)
    wait_for(w2, load_sem.at[5])
    for k in (2, 1, 3):
        weight_copy(k).start()
    wait_for(mask_v, load_sem.at[6])
    for p in range(wide):
        shared[p, 0] = (2 * mask_v[p]).astype(BF16)
    share_start(0, 0, 1, 2, 3, 4, 5, 6, 7)
    share_start(1, 0, 1, 2, 3, 4, 5, 6, 7)
    wait_for(self_term.at[:, 0], load_sem.at[4])
    for copy in loads[2:5]:
        copy.wait()
    me = r * blocks - 2 * blocks
    local = [jnp.clip(cols_s[s] - me, 0, 5 * blocks - 1) for s in range(slots)]
    for s in range(slots):
        live = s < count_s[0]
        for b in range(blocks):
            here = jnp.logical_and(live, rows_s[s] == b)
            keep = jnp.where(here, 1.0, 0.0).astype(BF16)
            placed[pl.ds(b * BS, BS), pl.ds(s * BS, BS)] = adj_v[s] * keep
    degree = jnp.dot(placed[...], jnp.ones((slots * BS, 2 * BS), BF16),
                     preferred_element_type=F32)
    scale[...] = lax.rsqrt(degree)

    def aggregate(stage):
        tiles = jnp.concatenate([ext[stage][i] for i in local], axis=0)
        summed = jnp.dot(placed[...], tiles, preferred_element_type=F32)
        return summed * scale[...]

    def own_rows(stage):
        return jnp.concatenate([ext[stage][2 * blocks + b] for b in range(blocks)], axis=0)

    def product(left, weight, k):
        return jnp.dot(left, weight[:, quarter(k)], preferred_element_type=F32)

    def matmul(left, right):
        return jnp.dot(left, right, preferred_element_type=F32)

    def self_project(stage, w_self):
        mine = own_rows(stage)
        for k in range(n_col):
            self_term[stage, k] = product(mine, w_self, k)

    def spread(stage, share):
        for k, sent in ((2, (0, 1, 2, 3)), (1, (9, 11)), (3, (8, 10)), (0, ())):
            term[stage, k] = share(k).astype(BF16)
            for i in sent:
                col_copy(stage, i).start()

    def spread_terms(row_stage, col_stage, w_neigh):
        row_wait(row_stage)
        agg = aggregate(row_stage).astype(BF16)
        spread(col_stage, lambda k: self_term[row_stage, k] + product(agg, w_neigh, k))

    def relay(stage, part):
        wait_for(mid.at[stage, tall_rows(part)], first_recv(stage, part))
        for j in (2 * part, 2 * part + 1):
            both_terms = (term[stage, onward(j), rows(j)].astype(F32)
                          + mid[stage, rows(j)].astype(F32))
            relayed[stage, rows(j)] = both_terms.astype(BF16)
            col_copy(stage, 4 + j).start()

    def gathered(stage, part):
        if stage == 0:
            wait_for(got.at[stage, :, tall_rows(part)], last_recv(stage, part))
        elif part == 0:
            wait_for(got.at[stage], last_recv(stage, part))
        here = tall_rows(part)
        return (term[stage, 0, here].astype(F32) + got[stage, 0, here].astype(F32)
                + got[stage, 1, here].astype(F32))

    self_project(0, ws1)
    wait_for(spread_w.at[odd, :, slim_rows], w_recv.at[0])
    pair_copy().start()
    spread_terms(0, 0, wn1)
    wait_for(spread_w.at[odd, :, slim_rows], w_recv.at[3])
    for by in (2, 1, 3):
        line_copy(by).start()
    for part in (0, 1):
        relay(0, part)
    share_forward(0)

    def send_dropped(p, part):
        kept = (shared[wide, 0, tall_rows(part)].astype(F32)
                * (2 * mask_v[p, tall_rows(part)]).astype(F32)).astype(BF16)
        for b in range(blocks // 2):
            ext[1 + p][2 * blocks + part * (blocks // 2) + b] = kept[b * BS:(b + 1) * BS]

    for part in (0, 1):
        shared[wide, 0, tall_rows(part)] = jnp.maximum(gathered(0, part), 0.0).astype(BF16)
        share_start(wide, 2 * part, 2 * part + 1)
        send_dropped(wide, part)
        row_start(1 + wide, part)
    share_start(wide, 4, 5, 6, 7)
    for p in narrow[1:]:
        for part in (0, 1):
            send_dropped(p, part)
        row_start_all(1 + p)
    share_forward(wide)
    share_forward(1)
    wait_for(spread_w.at[odd, :, pl.ds(0, 3 * piece)], w_recv.at[1])
    weight_forward().start()
    for p in narrow:
        self_project(1 + p, w2.at[0])

    def project_wide(p):
        share_wait(p)
        kept = [(shared[wide, k].astype(F32) * shared[p, k].astype(F32)).astype(BF16)
                for k in range(n_col)]

        def project(m):
            total = product(kept[0], w2.at[m], 0)
            for k in range(1, n_col):
                total = total + matmul(kept[k], spread_w[m, k - 1])
            return total

        value = project(1).astype(BF16)
        for b in range(blocks):
            ext[1 + p][2 * blocks + b] = value[b * BS:(b + 1) * BS]
        row_start_all(1 + p)
        self_wide[p] = project(0)

    for i, p in enumerate(narrow):
        spread_terms(1 + p, 1 + i, w2.at[1])
        if i == 0:
            share_wait(wide)
            weight_forward().wait_recv()
        project_wide(i)
    for i, p in enumerate(narrow):
        for part in (0, 1):
            relay(1 + i, part)
    for p in range(wide):
        row_wait(1 + p)
        out[p] = (self_wide[p] + aggregate(1 + p)).astype(BF16)
    for i, p in enumerate(narrow):
        for part in (0, 1):
            out[p, tall_rows(part)] = gathered(1 + i, part).astype(BF16)
    row_drain()
    wait_for(self_term.at[pl.ds(0, 3)], sent)


def interleave(stacked, out, held, sem):
    rows = stacked.shape[1]
    step, size = rows // 8, rows // CHUNKS
    copies = []
    for chunk in range(CHUNKS):
        for low in range(chunk * size, (chunk + 1) * size, step):
            part = stacked[:, low:low + step, :].astype(F32)
            held[low:low + step] = jnp.swapaxes(part, 0, 1).astype(BF16)
        span = pl.ds(chunk * size, size)
        copies.append(pltpu.make_async_copy(held.at[span], out.at[span], sem.at[chunk]))
        copies[-1].start()
    for copy in copies:
        copy.wait()


def solution(mesh):
    n_row, n_col = mesh.shape["row"], mesh.shape["col"]

    def on_device(features, masks, adj, adj_rows, adj_cols, adj_count, *weights):
        node_rows, width = features.shape
        blocks, slots, passes = node_rows // BS, adj_rows.shape[0], masks.shape[1]
        hidden = weights[0].shape[1]
        wide = passes // 2
        scatters = 1 + passes - wide
        dma = pltpu.SemaphoreType.DMA
        tile = (node_rows, width)
        ext = pltpu.VMEM((5 * blocks, BS, width), BF16)
        any_spec = pl.BlockSpec(memory_space=pl.ANY)
        vmem_spec = pl.BlockSpec(memory_space=pltpu.VMEM)
        stacked = pl.pallas_call(
            functools.partial(fused, n_row, n_col, passes, wide, blocks, slots),
            out_shape=pltpu.VMEM((passes,) + tile, BF16),
            in_specs=[any_spec] * 10,
            out_specs=vmem_spec,
            scratch_shapes=[
                pltpu.SMEM((slots,), jnp.int32), pltpu.SMEM((slots,), jnp.int32),
                pltpu.SMEM((1,), jnp.int32),
                pltpu.VMEM(adj.shape, BF16), pltpu.VMEM((node_rows, slots * BS), BF16),
                pltpu.VMEM(tile, F32),
                pltpu.VMEM((width, hidden), BF16), pltpu.VMEM((width, hidden), BF16),
                pltpu.VMEM((2, width, hidden), BF16),
                pltpu.VMEM((passes,) + tile, jnp.int32),
                pltpu.VMEM((1 + passes, n_col) + tile, F32),
                pltpu.VMEM((scatters, n_col) + tile, BF16),
                pltpu.VMEM((scatters,) + tile, BF16),
                pltpu.VMEM((scatters,) + tile, BF16),
                pltpu.VMEM((scatters, 2) + tile, BF16),
                pltpu.VMEM((2, n_col - 1) + tile, BF16),
                pltpu.VMEM((1 + wide, n_col) + tile, BF16),
                pltpu.VMEM((wide,) + tile, F32),
            ] + [ext] * (1 + passes) + [
                dma((7,)), dma((2,)), dma((1 + passes,)), dma((1 + passes,)), dma(()),
                dma((3 * scatters + 1,)), dma((2 * wide + 3,)), dma((4,)),
            ],
            compiler_params=pltpu.CompilerParams(
                collective_id=0, has_side_effects=True, vmem_limit_bytes=48 * 2**20),
        )(*[pltpu.with_memory_space_constraint(x, pltpu.HBM) if x.size > 1 else x for x in (
            features.reshape(blocks, BS, width), masks, adj, adj_rows, adj_cols, adj_count, *weights)])
        return pl.pallas_call(
            interleave,
            out_shape=jax.ShapeDtypeStruct((node_rows, passes, width), BF16),
            in_specs=[vmem_spec],
            out_specs=any_spec,
            scratch_shapes=[pltpu.VMEM((node_rows, passes, width), BF16), dma((CHUNKS,))],
            compiler_params=pltpu.CompilerParams(vmem_limit_bytes=16 * 2**20),
        )(stacked)

    in_specs = (
        P("row", "col"), P("row", None, "col"), P("row", None, None), P("row"), P("row"),
        P("row"), P("col", None), P("col", None), P("col", None), P("col", None),
    )
    return jax.shard_map(on_device, mesh=mesh, in_specs=in_specs,
                         out_specs=P("row", None, "col"), check_vma=False)
```

```python
import functools

import jax
import jax.numpy as jnp
from jax import lax
from jax.experimental import pallas as pl
from jax.experimental.pallas import tpu as pltpu
from jax.sharding import PartitionSpec as P

BS = 128
LINE = 4
CHUNKS = 8
MESH = pl.DeviceIdType.MESH
BF16, F32 = jnp.bfloat16, jnp.float32


def fused(n_row, n_col, passes, wide, blocks, slots, *refs):
    (features, masks, adj, adj_rows, adj_cols, adj_count, w_self_one, w_neigh_one,
     w_self_two, w_neigh_two, out) = refs[:11]
    rest = list(refs[11:])
    rows_s, cols_s, count_s, adj_v, placed, scale, ws1, wn1, w2, mask_v = rest[:10]
    self_term, term, mid, relayed, got, spread_w, shared, self_wide = rest[10:18]
    ext = rest[18:19 + passes]
    (load_sem, row_send, far_recv, near_recv, sent, col_recv, share_recv,
     w_recv) = rest[19 + passes:]

    r, c = lax.axis_index("row"), lax.axis_index("col")
    odd = lax.rem(r, 2)
    has_left, has_right = r >= 2, r < n_row - 2
    inner = jnp.where(odd == 0, has_right, has_left)
    outer = jnp.where(odd == 0, has_left, has_right)
    sibling = (r + 1 - 2 * odd, c)
    far_right, far_left = (lax.rem(r + 2, n_row), c), (lax.rem(r + n_row - 2, n_row), c)
    across = (r - 1 + 2 * odd, c)
    col_right, col_left = (r, lax.rem(c + 1, n_col)), (r, lax.rem(c + n_col - 1, n_col))
    narrow = range(wide, passes)
    scatters = 1 + len(narrow)
    mixed = [stage in (0, wide, 1 + wide) for stage in range(1 + passes)]
    col_across = (r, lax.rem(c + 2, n_col))
    node_rows = blocks * BS
    piece, tall = node_rows // 4, node_rows // 2
    line = 2 * LINE
    spot, upper = lax.rem(r // 2, LINE), lax.rem(r // (2 * LINE), 2)
    paired = (r + line * (1 - 2 * upper), c)

    barrier = pltpu.get_barrier_semaphore()

    def greet(device):
        pl.semaphore_signal(barrier, 1, device_id=device, device_id_type=MESH)

    pl.when(has_right)(lambda: greet(far_right))
    pl.when(has_left)(lambda: greet(far_left))
    pl.when(outer)(lambda: greet(across))
    def along_line(by):
        return (r - lax.rem(r, line) + lax.rem(r + 2 * by, line), c)

    for device in (sibling, col_right, col_left, col_across, paired) + tuple(
            along_line(by) for by in range(1, LINE)):
        greet(device)

    loads = []
    own = ext[0].at[pl.ds(2 * blocks, blocks)]
    for i, src, dst in (
        (0, features, own), (4, adj, adj_v), (1, adj_rows, rows_s), (2, adj_cols, cols_s),
        (3, adj_count, count_s), (4, w_self_one, ws1), (4, w_neigh_one, wn1),
        (5, w_self_two, w2.at[0]), (5, w_neigh_two, w2.at[1]),
    ):
        loads.append(pltpu.make_async_copy(src, dst, load_sem.at[i]))
    mask_loads = [
        pltpu.make_async_copy(masks.at[:, p, :], mask_v.at[p], load_sem.at[6])
        for p in range(passes)
    ]

    def wait_for(ref, sem):
        pltpu.make_async_copy(ref, ref, sem).wait()

    for copy in loads + mask_loads:
        copy.start()
    loads[0].wait()
    peers = sum(flag.astype(jnp.int32) for flag in (has_left, has_right, outer))
    pl.semaphore_wait(barrier, 4 + LINE + peers)

    def remote(src, dst, send, recv, device):
        return pltpu.make_async_remote_copy(
            src_ref=src, dst_ref=dst, send_sem=send, recv_sem=recv, device_id=device,
            device_id_type=MESH)

    def row_copy(stage, i, part):
        src, dst, device = (
            (2, 0, far_right), (2, 4, far_left), (2, 1 + 2 * odd, sibling),
            (4 - 4 * odd, 3 - 2 * odd, sibling), (2, 3 - 2 * odd, across))[i]
        size = blocks // 2 if mixed[stage] else blocks
        pairs = [ext[stage].at[pl.ds(n * blocks + part * size, size)] for n in (src, dst)]
        recv = far_recv.at[stage] if i < 2 and not part else near_recv.at[stage]
        return remote(*pairs, row_send.at[0 if mixed[stage] else 1], recv, device)

    def row_start(stage, part):
        pl.when(has_right)(lambda: row_copy(stage, 0, part).start())
        pl.when(has_left)(lambda: row_copy(stage, 1, part).start())
        if part:
            pl.when(outer)(lambda: row_copy(stage, 4, part).start())
        row_copy(stage, 2, part).start()

    def row_start_all(stage):
        for part in range(1 + mixed[stage]):
            row_start(stage, part)

    def one_of(flag, stage, many, few, sem):
        pl.when(flag)(lambda: wait_for(ext[stage].at[pl.ds(0, many)], sem))
        pl.when(jnp.logical_not(flag))(lambda: wait_for(ext[stage].at[pl.ds(0, few)], sem))

    both = jnp.logical_and(has_left, has_right)

    def row_wait(stage):
        size = blocks // 2 if mixed[stage] else blocks
        one_of(both, stage, 2 * size, size, far_recv.at[stage])
        pl.when(inner)(lambda: row_copy(stage, 3, 0).start())
        if not mixed[stage]:
            one_of(outer, stage, 2 * blocks, blocks, near_recv.at[stage])
            return
        pl.when(both)(lambda: wait_for(ext[stage].at[pl.ds(0, 6 * size)], near_recv.at[stage]))

        @pl.when(jnp.logical_not(both))
        def _():
            one_of(outer, stage, 5 * size, 3 * size, near_recv.at[stage])

    def row_drain():
        def drained(stages, blocks_each, sem):
            wait_for(self_term.at[pl.ds(0, stages), pl.ds(0, blocks_each), pl.ds(0, BS // 2)],
                     sem)

        some = sum(mixed)
        others = len(mixed) - some

        @pl.when(both)
        def _():
            whole = self_term.at[pl.ds(0, some), :, pl.ds(0, BS)]
            wait_for(whole, row_send.at[0])
            drained(2 * others, 4, row_send.at[1])

        @pl.when(jnp.logical_not(both))
        def _():
            drained(5, some, row_send.at[0])
            pl.when(inner)(lambda: drained(others + 1, 4, row_send.at[1]))
            pl.when(jnp.logical_not(inner))(lambda: drained(others, 4, row_send.at[1]))

    def rows(j):
        return pl.ds(j * piece, piece)

    def toward(j):
        return (col_right, col_left)[j % 2]

    def onward(j):
        return (1, 3)[j % 2]

    def first_recv(stage, part):
        return col_recv.at[3 * stage + part]

    def last_recv(stage, part):
        return col_recv.at[3 * stage + 2 if stage or not part else 3 * scatters]

    def col_copy(stage, i):
        t, g = term.at[stage], got.at[stage]
        j = i % 4
        if i < 4:
            src, dst, device = t.at[2, rows(j)], mid.at[stage, rows(j)], toward(j)
        elif i < 8:
            src, dst, device = relayed.at[stage, rows(j)], g.at[j % 2, rows(j)], toward(j)
        else:
            k = 4 - onward(j)
            src, dst, device = t.at[k, rows(j)], g.at[1 - j % 2, rows(j)], toward(j + 1)
        recv = first_recv(stage, j // 2) if i < 4 else last_recv(stage, j // 2)
        return remote(src, dst, sent, recv, device)

    def shared_recv(stage, n):
        if stage < wide:
            return share_recv.at[2 * stage + n // 2]
        return share_recv.at[2 * wide + n]

    def share_copy(stage, i):
        held = shared.at[stage]
        j = i % 4
        if i < 4:
            src, dst, device = 0, onward(j), toward(j)
        elif i < 8:
            src, dst, device = 0, 4 - onward(j), toward(j + 1)
        else:
            src, dst, device = onward(j), 2, toward(j)
        return remote(held.at[src, rows(j)], held.at[dst, rows(j)], sent,
                      shared_recv(stage, j // 2 if i < 4 else 2), device)

    def share_start(stage, *which):
        for i in which:
            share_copy(stage, i).start()

    def tall_rows(part):
        return pl.ds(part * tall, tall)

    def share_forward(stage):
        if stage < wide:
            wait_for(shared.at[stage, 1], shared_recv(stage, 0))
            share_start(stage, 8, 9, 10, 11)
            return
        for part in (0, 1):
            wait_for(shared.at[stage, 1, tall_rows(part)], shared_recv(stage, part))
            share_start(stage, 8 + 2 * part, 9 + 2 * part)

    def share_wait(stage):
        wait_for(shared.at[stage, pl.ds(1, 2)], shared_recv(stage, 2))

    def quarter(k):
        return pl.ds(pl.multiple_of(lax.rem(c + k, n_col) * node_rows, node_rows), node_rows)

    part_rows = pl.ds(pl.multiple_of(spot * piece, piece), piece)

    slim = piece // 2
    slim_rows = pl.ds(pl.multiple_of(spot * piece + upper * slim, slim), slim)

    def weight_copy(k):
        device = {1: col_right, 2: col_across, 3: col_left}[k]
        return remote(w2.at[odd, slim_rows, quarter(k)], spread_w.at[odd, k - 1, slim_rows],
                      sent, w_recv.at[0], device)

    def pair_copy():
        part = spread_w.at[odd, :, slim_rows]
        return remote(part, part, sent, w_recv.at[3], paired)

    def line_copy(by):
        part = spread_w.at[odd, :, part_rows]
        return remote(part, part, sent, w_recv.at[1], along_line(by))

    def weight_forward():
        blocks_held = spread_w.at[odd]
        return remote(blocks_held, blocks_held, sent, w_recv.at[2], sibling)

    row_start_all(0)
    wait_for(w2, load_sem.at[5])
    for k in (2, 1, 3):
        weight_copy(k).start()
    wait_for(mask_v, load_sem.at[6])
    for p in range(wide):
        shared[p, 0] = (2 * mask_v[p]).astype(BF16)
    share_start(0, 0, 1, 2, 3, 4, 5, 6, 7)
    share_start(1, 0, 1, 2, 3, 4, 5, 6, 7)
    wait_for(self_term.at[:, 0], load_sem.at[4])
    for copy in loads[2:5]:
        copy.wait()
    me = r * blocks - 2 * blocks
    local = [jnp.clip(cols_s[s] - me, 0, 5 * blocks - 1) for s in range(slots)]
    for s in range(slots):
        live = s < count_s[0]
        for b in range(blocks):
            here = jnp.logical_and(live, rows_s[s] == b)
            keep = jnp.where(here, 1.0, 0.0).astype(BF16)
            placed[pl.ds(b * BS, BS), pl.ds(s * BS, BS)] = adj_v[s] * keep
    degree = jnp.dot(placed[...], jnp.ones((slots * BS, 2 * BS), BF16),
                     preferred_element_type=F32)
    scale[...] = lax.rsqrt(degree)

    def aggregate(stage):
        tiles = jnp.concatenate([ext[stage][i] for i in local], axis=0)
        summed = jnp.dot(placed[...], tiles, preferred_element_type=F32)
        return summed * scale[...]

    def own_rows(stage):
        return jnp.concatenate([ext[stage][2 * blocks + b] for b in range(blocks)], axis=0)

    def product(left, weight, k):
        return jnp.dot(left, weight[:, quarter(k)], preferred_element_type=F32)

    def matmul(left, right):
        return jnp.dot(left, right, preferred_element_type=F32)

    def self_project(stage, w_self):
        mine = own_rows(stage)
        for k in range(n_col):
            self_term[stage, k] = product(mine, w_self, k)

    def spread(stage, share):
        for k, sent in ((2, (0, 1, 2, 3)), (1, (9, 11)), (3, (8, 10)), (0, ())):
            term[stage, k] = share(k).astype(BF16)
            for i in sent:
                col_copy(stage, i).start()

    def spread_terms(row_stage, col_stage, w_neigh):
        row_wait(row_stage)
        agg = aggregate(row_stage).astype(BF16)
        spread(col_stage, lambda k: self_term[row_stage, k] + product(agg, w_neigh, k))

    def relay(stage, part):
        wait_for(mid.at[stage, tall_rows(part)], first_recv(stage, part))
        for j in (2 * part, 2 * part + 1):
            both_terms = (term[stage, onward(j), rows(j)].astype(F32)
                          + mid[stage, rows(j)].astype(F32))
            relayed[stage, rows(j)] = both_terms.astype(BF16)
            col_copy(stage, 4 + j).start()

    def gathered(stage, part):
        if stage == 0:
            wait_for(got.at[stage, :, tall_rows(part)], last_recv(stage, part))
        elif part == 0:
            wait_for(got.at[stage], last_recv(stage, part))
        here = tall_rows(part)
        return (term[stage, 0, here].astype(F32) + got[stage, 0, here].astype(F32)
                + got[stage, 1, here].astype(F32))

    self_project(0, ws1)
    wait_for(spread_w.at[odd, :, slim_rows], w_recv.at[0])
    pair_copy().start()
    spread_terms(0, 0, wn1)
    wait_for(spread_w.at[odd, :, slim_rows], w_recv.at[3])
    for by in (2, 1, 3):
        line_copy(by).start()
    for part in (0, 1):
        relay(0, part)
    share_forward(0)

    def send_dropped(p, part):
        kept = (shared[wide, 0, tall_rows(part)].astype(F32)
                * (2 * mask_v[p, tall_rows(part)]).astype(F32)).astype(BF16)
        for b in range(blocks // 2):
            ext[1 + p][2 * blocks + part * (blocks // 2) + b] = kept[b * BS:(b + 1) * BS]

    for part in (0, 1):
        shared[wide, 0, tall_rows(part)] = jnp.maximum(gathered(0, part), 0.0).astype(BF16)
        share_start(wide, 2 * part, 2 * part + 1)
        send_dropped(wide, part)
        row_start(1 + wide, part)
    share_start(wide, 4, 5, 6, 7)
    for p in narrow[1:]:
        for part in (0, 1):
            send_dropped(p, part)
        row_start_all(1 + p)
    share_forward(wide)
    share_forward(1)
    wait_for(spread_w.at[odd, :, pl.ds(0, 3 * piece)], w_recv.at[1])
    weight_forward().start()
    for p in narrow:
        self_project(1 + p, w2.at[0])

    def project_wide(p):
        share_wait(p)
        kept = [(shared[wide, k].astype(F32) * shared[p, k].astype(F32)).astype(BF16)
                for k in range(n_col)]

        def project(m):
            total = product(kept[0], w2.at[m], 0)
            for k in range(1, n_col):
                total = total + matmul(kept[k], spread_w[m, k - 1])
            return total

        value = project(1).astype(BF16)
        for b in range(blocks):
            ext[1 + p][2 * blocks + b] = value[b * BS:(b + 1) * BS]
        row_start_all(1 + p)
        self_wide[p] = project(0)

    for i, p in enumerate(narrow):
        spread_terms(1 + p, 1 + i, w2.at[1])
        if i == 0:
            share_wait(wide)
            weight_forward().wait_recv()
        project_wide(i)
    for i, p in enumerate(narrow):
        for part in (0, 1):
            relay(1 + i, part)
    for p in range(wide):
        row_wait(1 + p)
        out[p] = (self_wide[p] + aggregate(1 + p)).astype(BF16)
    for i, p in enumerate(narrow):
        for part in (0, 1):
            out[p, tall_rows(part)] = gathered(1 + i, part).astype(BF16)
    row_drain()
    wait_for(self_term.at[pl.ds(0, 3)], sent)


def interleave(stacked, out, held, sem):
    rows = stacked.shape[1]
    step, size = rows // 8, rows // CHUNKS
    copies = []
    for chunk in range(CHUNKS):
        for low in range(chunk * size, (chunk + 1) * size, step):
            part = stacked[:, low:low + step, :].astype(F32)
            held[low:low + step] = jnp.swapaxes(part, 0, 1).astype(BF16)
        span = pl.ds(chunk * size, size)
        copies.append(pltpu.make_async_copy(held.at[span], out.at[span], sem.at[chunk]))
        copies[-1].start()
    for copy in copies:
        copy.wait()


def solution(mesh):
    n_row, n_col = mesh.shape["row"], mesh.shape["col"]

    def on_device(features, masks, adj, adj_rows, adj_cols, adj_count, *weights):
        node_rows, width = features.shape
        blocks, slots, passes = node_rows // BS, adj_rows.shape[0], masks.shape[1]
        hidden = weights[0].shape[1]
        wide = passes // 2
        scatters = 1 + passes - wide
        dma = pltpu.SemaphoreType.DMA
        tile = (node_rows, width)
        ext = pltpu.VMEM((5 * blocks, BS, width), BF16)
        any_spec = pl.BlockSpec(memory_space=pl.ANY)
        vmem_spec = pl.BlockSpec(memory_space=pltpu.VMEM)
        stacked = pl.pallas_call(
            functools.partial(fused, n_row, n_col, passes, wide, blocks, slots),
            out_shape=pltpu.VMEM((passes,) + tile, BF16),
            in_specs=[any_spec] * 10,
            out_specs=vmem_spec,
            scratch_shapes=[
                pltpu.SMEM((slots,), jnp.int32), pltpu.SMEM((slots,), jnp.int32),
                pltpu.SMEM((1,), jnp.int32),
                pltpu.VMEM(adj.shape, BF16), pltpu.VMEM((node_rows, slots * BS), BF16),
                pltpu.VMEM(tile, F32),
                pltpu.VMEM((width, hidden), BF16), pltpu.VMEM((width, hidden), BF16),
                pltpu.VMEM((2, width, hidden), BF16),
                pltpu.VMEM((passes,) + tile, jnp.int32),
                pltpu.VMEM((1 + passes, n_col) + tile, F32),
                pltpu.VMEM((scatters, n_col) + tile, BF16),
                pltpu.VMEM((scatters,) + tile, BF16),
                pltpu.VMEM((scatters,) + tile, BF16),
                pltpu.VMEM((scatters, 2) + tile, BF16),
                pltpu.VMEM((2, n_col - 1) + tile, BF16),
                pltpu.VMEM((1 + wide, n_col) + tile, BF16),
                pltpu.VMEM((wide,) + tile, F32),
            ] + [ext] * (1 + passes) + [
                dma((7,)), dma((2,)), dma((1 + passes,)), dma((1 + passes,)), dma(()),
                dma((3 * scatters + 1,)), dma((2 * wide + 3,)), dma((4,)),
            ],
            compiler_params=pltpu.CompilerParams(
                collective_id=0, has_side_effects=True, vmem_limit_bytes=48 * 2**20),
        )(*[pltpu.with_memory_space_constraint(x, pltpu.HBM) if x.size > 1 else x for x in (
            features.reshape(blocks, BS, width), masks, adj, adj_rows, adj_cols, adj_count, *weights)])
        return pl.pallas_call(
            interleave,
            out_shape=jax.ShapeDtypeStruct((node_rows, passes, width), BF16),
            in_specs=[vmem_spec],
            out_specs=any_spec,
            scratch_shapes=[pltpu.VMEM((node_rows, passes, width), BF16), dma((CHUNKS,))],
            compiler_params=pltpu.CompilerParams(vmem_limit_bytes=16 * 2**20),
        )(stacked)

    in_specs = (
        P("row", "col"), P("row", None, "col"), P("row", None, None), P("row"), P("row"),
        P("row"), P("col", None), P("col", None), P("col", None), P("col", None),
    )
    return jax.shard_map(on_device, mesh=mesh, in_specs=in_specs,
                         out_specs=P("row", None, "col"), check_vma=False)
```
